512 devices in a mesh: ctx: 64 (over x, z), tp: 8 (over y, core).
Axes of the slice: x: 4, y: 4, z: 16, core: 2. Of those that a mesh axis runs over, the one named last changes fastest.
Arguments:
- queries: bfloat16 [65536, 4096], P('ctx', 'tp'), may hold values from -6 to 6
- keys: bfloat16 [65536, 4096], P('ctx', 'tp'), may hold values from -6 to 6
- values: bfloat16 [65536, 4096], P('ctx', 'tp'), may hold values from -23 to 23
- gain: float32 [4096], P('tp'), may hold values from 0.5 to 1.5
Outputs:
- scored: bfloat16 [65536, 4096], P('ctx', 'tp')
The draws below stay inside these ranges and needn't reach their ends.
All inputs are finite; a program needn't handle non-finite values.
Results may differ from the reference program's by a relative error of at most 0.0049.
Values sent between devices are 32-bit elements; how exact they have to be, the bound alone decides.
No kernel may reach another device: no remote copies, remote signals or barrier semaphores. Data moves between devices by JAX's collectives and lax.ppermute only.
A program may use at most 64 MiB of HBM per device.

```python
import jax
import jax.numpy as jnp
from jax import lax

HEADS = 32
HD = 128
D = 4096
BLOCK = 512
TOKENS = 65536


def draw_values(key, part):
    key = jax.random.fold_in(key, 7)
    first, second = jax.random.split(key)
    column_head = jnp.arange(HEADS * HD) // HD
    ramp = 1.0 + 2.0 * column_head.astype(jnp.float32) / (HEADS - 1)
    base = jnp.clip(jax.random.normal(first, (TOKENS, HEADS * HD), jnp.float32), -6.0, 6.0)
    factor = jax.random.uniform(second, (HEADS,), jnp.float32, 0.8, 1.25)
    head_factor = jnp.take(factor, column_head)
    return (base * ramp[None, :] * head_factor[None, :]).astype(jnp.bfloat16)


def level_of(own_key, shape, pieces, low, largest):
    level, own = 1.0, jax.random.fold_in(own_key, 6)
    for axis_at, parts in pieces:
        steps = jnp.exp(jax.random.uniform(jax.random.fold_in(own, axis_at), (parts,), jnp.float32, low / len(pieces), largest / len(pieces)))
        level = level * jnp.repeat(steps, shape[axis_at] // parts).reshape([-1 if axis == axis_at else 1 for axis in range(len(shape))])
    return level


def centred(stream_key, dims, deviation, limit, cuts=(), held_as=jnp.bfloat16):
    array = deviation * jax.random.normal(stream_key, dims, jnp.float32)
    if cuts:
        array = array * level_of(stream_key, dims, cuts, -0.22, 0.18)
    return jnp.clip(array, -limit, limit).astype(held_as)


def setup_inputs(seed: int = 0) -> dict:
    splits = jax.random.split(jax.random.key(seed), 5)
    return {
        "queries": centred(splits[0], (TOKENS, D), 1.0, 6.0, ((0, 64), (1, 8))),
        "keys": centred(splits[1], (TOKENS, D), 1.0, 6.0, ((0, 64), (1, 8))),
        "values": draw_values(jax.random.fold_in(splits[4], 71), 0),
        "gain": jnp.clip(1.0 + 0.1 * jax.random.normal(splits[3], (D,), jnp.float32), 0.5, 1.5),
    }


def reference(queries, keys, values, gain):
    count = queries.shape[0] // BLOCK
    qs = queries.reshape(count, BLOCK, HEADS, HD)
    ks = keys.reshape(count, BLOCK, HEADS, HD)
    vs = values.reshape(count, BLOCK, HEADS, HD)
    lower = (jnp.arange(BLOCK)[:, None] >= jnp.arange(BLOCK)[None, :]).astype(jnp.float32)

    def step(state, blocks):
        qb, kb, vb = blocks
        qf = qb.astype(jnp.float32)
        kf = kb.astype(jnp.float32)
        vf = vb.astype(jnp.float32)
        low = lax.optimization_barrier(state.astype(jnp.bfloat16)).astype(jnp.float32)
        carried = jnp.einsum('thd,hde->the', qf, low)
        scores = jnp.einsum('thd,shd->hts', qf, kf) * lower[None]
        scores = lax.optimization_barrier(scores.astype(jnp.bfloat16)).astype(jnp.float32)
        local = jnp.einsum('hts,she->the', scores, vf)
        mixed = (carried + local).reshape(BLOCK, D)
        meansq = lax.optimization_barrier(jnp.mean(mixed * mixed, axis=1, keepdims=True))
        scored = (mixed / jnp.sqrt(meansq + 1e-06) * gain[None, :]).astype(jnp.bfloat16)
        newstate = state + jnp.einsum('thd,the->hde', kf, vf)
        return (newstate, scored)
    start = jnp.zeros((HEADS, HD, HD), jnp.float32)
    final, outputs = lax.scan(step, start, (qs, ks, vs))
    return outputs.reshape(count * BLOCK, D)
```

```python
import jax
import jax.numpy as jnp
from jax import lax
from jax.sharding import PartitionSpec as P

HD = 128
D = 4096
BLOCK = 512
XS = 4
ZS = 16
NEAR = 4
FAR = ZS // NEAR


def near_groups():
    return [[x * ZS + a * NEAR + b for x in range(XS) for b in range(NEAR)] for a in range(FAR)]


def far_groups():
    return [[x * ZS + a * NEAR + b for a in range(FAR)] for x in range(XS) for b in range(NEAR)]


def exclusive_states(state):
    heads = state.shape[0]
    members = XS * NEAR
    pieces = state.reshape(members, heads * HD // members, HD)
    got = lax.all_to_all(pieces, "ctx", 0, 0, axis_index_groups=near_groups())
    rows = got.reshape(XS, NEAR, *got.shape[1:])
    mine = (lax.axis_index("ctx") % ZS) // NEAR
    group = jnp.sum(rows, axis=1)
    earlier_rows = jnp.cumsum(group, axis=0) - group
    later = (mine < jnp.arange(FAR)).astype(jnp.float32)
    sent = earlier_rows[None] + later[:, None, None, None] * group[None]
    parts = lax.all_to_all(sent, "ctx", 0, 0, axis_index_groups=far_groups())
    start = jnp.sum(parts, axis=0)
    running = [start]
    for b in range(NEAR - 1):
        running.append(running[-1] + rows[:, b])
    back = jnp.stack(running, axis=1).reshape(got.shape)
    mine_back = lax.all_to_all(back, "ctx", 0, 0, axis_index_groups=near_groups())
    return mine_back.reshape(state.shape)


def shards(queries, keys, values, gain):
    tok_rows = queries.shape[0]
    heads_here = queries.shape[1] // HD
    count = tok_rows // BLOCK
    qs = queries.reshape(count, BLOCK, heads_here, HD)
    ks = keys.reshape(count, BLOCK, heads_here, HD)
    vs = values.reshape(count, BLOCK, heads_here, HD)
    block_state = jnp.einsum("bthd,bthe->bhde", ks, vs, preferred_element_type=jnp.float32)
    shard_state = jnp.sum(block_state, axis=0)
    carried_in = exclusive_states(shard_state)
    running = jnp.stack([jnp.zeros_like(block_state[0]), block_state[0]])
    prefix_low = (carried_in[None] + running).astype(jnp.bfloat16)
    carried = jnp.einsum("bthd,bhde->bthe", qs, prefix_low, preferred_element_type=jnp.float32)
    lower = jnp.arange(BLOCK)[:, None] >= jnp.arange(BLOCK)[None, :]
    scores = jnp.einsum("bthd,bshd->bhts", qs, ks, preferred_element_type=jnp.float32)
    scores = jnp.where(lower[None, None], scores, 0.0).astype(jnp.bfloat16)
    local = jnp.einsum("bhts,bshe->bthe", scores, vs, preferred_element_type=jnp.float32)
    mixed = (carried + local).reshape(tok_rows, heads_here * HD)
    partial_sq = jnp.sum(mixed * mixed, axis=1)
    peers = lax.axis_size("tp")
    copies = jnp.broadcast_to(partial_sq[None], (peers, tok_rows))
    total_sq = jnp.sum(lax.all_to_all(copies, "tp", 0, 0), axis=0)
    meansq = total_sq / D
    scored = mixed / jnp.sqrt(meansq + 1e-06)[:, None] * gain[None, :]
    return scored.astype(jnp.bfloat16)


def solution(mesh):
    return jax.shard_map(
        shards,
        mesh=mesh,
        in_specs=(P("ctx", "tp"), P("ctx", "tp"), P("ctx", "tp"), P("tp")),
        out_specs=P("ctx", "tp"),
        check_vma=False,
    )
```

```python
import jax
import jax.numpy as jnp
from jax import lax
from jax.experimental import pallas as pl
from jax.experimental.pallas import tpu as pltpu
from jax.sharding import PartitionSpec as P

HD = 128
D = 4096
BLOCK = 512
XS = 4
ZS = 16
NEAR = 4
FAR = ZS // NEAR
MEMBERS = XS * NEAR
PEERS = 8
LOAD = 128
CHUNK = 256
STORE = 128
VMEM = pl.BlockSpec(memory_space=pltpu.VMEM)
HBM = pl.BlockSpec(memory_space=pltpu.HBM)
STATE_MIB = 53.2
MIXED_MIB = 32
OTHER_MIB = 32


def grant(mib):
    return pltpu.CompilerParams(vmem_limit_bytes=int(mib * 1024 * 1024))


def near_groups():
    return [[x * ZS + a * NEAR + b for x in range(XS) for b in range(NEAR)] for a in range(FAR)]


def far_groups():
    return [[x * ZS + a * NEAR + b for a in range(FAR)] for x in range(XS) for b in range(NEAR)]


def contract_tokens(left, right):
    return lax.dot_general(left, right, (((0,), (0,)), ((), ())), preferred_element_type=jnp.float32)


def contract_last(left, right):
    return lax.dot_general(left, right, (((1,), (1,)), ((), ())), preferred_element_type=jnp.float32)


def head_columns(h):
    return slice(h * HD, (h + 1) * HD)


def state_kernel(keys, values, total, key_rows, value_rows, sems):
    rows, width = keys.shape
    parts = rows // LOAD
    copies = []
    for c in range(parts):
        at = pl.ds(c * LOAD, LOAD)
        pair = (
            pltpu.make_async_copy(keys.at[at], key_rows.at[at], sems.at[c]),
            pltpu.make_async_copy(values.at[at], value_rows.at[at], sems.at[parts + c]),
        )
        for copy in pair:
            copy.start()
        copies.append(pair)
    sums = [None] * (width // HD)
    for c in range(0, rows, CHUNK):
        for pair in copies[c // LOAD : (c + CHUNK) // LOAD]:
            for copy in pair:
                copy.wait()
        for h in range(len(sums)):
            cols = head_columns(h)
            part = contract_tokens(key_rows[c : c + CHUNK, cols], value_rows[c : c + CHUNK, cols])
            sums[h] = part if c == 0 else sums[h] + part
    for h, s in enumerate(sums):
        total[h] = s


def shard_state(keys, values):
    rows, width = keys.shape
    return pl.pallas_call(
        state_kernel,
        in_specs=[HBM, HBM],
        out_specs=VMEM,
        out_shape=jax.ShapeDtypeStruct((width // HD, HD, HD), jnp.float32),
        scratch_shapes=[
            pltpu.VMEM((rows, width), keys.dtype),
            pltpu.VMEM((rows, width), values.dtype),
            pltpu.SemaphoreType.DMA((2 * rows // LOAD,)),
        ],
        compiler_params=grant(STATE_MIB),
        cost_estimate=pl.CostEstimate(flops=2 * rows * width * HD, bytes_accessed=4 * rows * width, transcendentals=0),
        name="states",
    )(keys, values)


def sent_kernel(got, sent):
    mine = (lax.axis_index("ctx") // NEAR) % FAR
    group, earlier = [], []
    for x in range(XS):
        g = got[x * NEAR]
        for b in range(1, NEAR):
            g = g + got[x * NEAR + b]
        group.append(g)
    e = jnp.zeros_like(group[0])
    for x in range(XS):
        earlier.append(e)
        e = e + group[x]
    for a in range(FAR):
        later = jnp.where(mine < a, 1.0, 0.0).astype(jnp.float32)
        for x in range(XS):
            sent[a, x] = earlier[x] + later * group[x]


def back_kernel(parts, got, back):
    for x in range(XS):
        run = parts[0, x]
        for a in range(1, FAR):
            run = run + parts[a, x]
        for b in range(NEAR):
            back[x * NEAR + b] = run
            if b < NEAR - 1:
                run = run + got[x * NEAR + b]


def exclusive_states(state):
    rows = state.shape[0] * HD // MEMBERS
    pieces = state.reshape(MEMBERS, rows, HD)
    got = lax.all_to_all(pieces, "ctx", 0, 0, axis_index_groups=near_groups())
    sent = pl.pallas_call(
        sent_kernel,
        in_specs=[VMEM],
        out_specs=VMEM,
        out_shape=jax.ShapeDtypeStruct((FAR, XS, rows, HD), jnp.float32),
        compiler_params=grant(OTHER_MIB),
        name="sent",
    )(got)
    parts = lax.all_to_all(sent, "ctx", 0, 0, axis_index_groups=far_groups())
    back = pl.pallas_call(
        back_kernel,
        in_specs=[VMEM, VMEM],
        out_specs=VMEM,
        out_shape=jax.ShapeDtypeStruct(got.shape, jnp.float32),
        compiler_params=grant(OTHER_MIB),
        name="back",
    )(parts, got)
    mine = lax.all_to_all(back, "ctx", 0, 0, axis_index_groups=near_groups())
    return mine.reshape(state.shape)


def mixed_kernel(queries, keys, values, prefix, mixed, squares):
    half = BLOCK // 2
    tiles = BLOCK // HD
    row = lax.broadcasted_iota(jnp.int32, (half, half), 0)
    col = lax.broadcasted_iota(jnp.int32, (half, half), 1)
    lower = row >= col
    for start in range(0, queries.shape[0], BLOCK):
        top_rows = slice(start, start + half)
        low_rows = slice(start + half, start + BLOCK)
        acc = [None, None]
        for h in range(queries.shape[1] // HD):
            cols = head_columns(h)
            state = prefix[h]
            if start:
                state = state + contract_tokens(keys[:start, cols], values[:start, cols])
            state = state.astype(jnp.bfloat16)
            q, k = queries[top_rows, cols], keys[top_rows, cols]
            top = jnp.where(lower, contract_last(q, k), 0.0).astype(jnp.bfloat16)
            m = jnp.dot(q, state, preferred_element_type=jnp.float32)
            m = m + jnp.dot(top, values[top_rows, cols], preferred_element_type=jnp.float32)
            mixed[top_rows, cols] = m
            acc[0] = m * m if h == 0 else acc[0] + m * m
            q = queries[low_rows, cols]
            side = contract_last(q, k).astype(jnp.bfloat16)
            low = jnp.where(lower, contract_last(q, keys[low_rows, cols]), 0.0).astype(jnp.bfloat16)
            both = jnp.concatenate([side, low], axis=1)
            m = jnp.dot(q, state, preferred_element_type=jnp.float32)
            m = m + jnp.dot(both, values[start : start + BLOCK, cols], preferred_element_type=jnp.float32)
            mixed[low_rows, cols] = m
            acc[1] = m * m if h == 0 else acc[1] + m * m
        for i, a in enumerate(acc):
            turned = jnp.swapaxes(a.reshape(tiles // 2, HD, HD), 1, 2)
            sums = jnp.sum(turned, axis=1)
            at = start // HD + i * (tiles // 2)
            for p in range(PEERS):
                squares[p, at : at + tiles // 2] = sums


def mixed_part(queries, keys, values, prefix):
    rows, width = queries.shape
    return pl.pallas_call(
        mixed_kernel,
        in_specs=[VMEM] * 4,
        out_specs=[VMEM] * 2,
        out_shape=[
            jax.ShapeDtypeStruct((rows, width), jnp.float32),
            jax.ShapeDtypeStruct((PEERS, rows // HD, HD), jnp.float32),
        ],
        compiler_params=grant(MIXED_MIB),
        cost_estimate=pl.CostEstimate(flops=4 * rows * BLOCK * width, bytes_accessed=10 * rows * width, transcendentals=0),
        name="mixed",
    )(queries, keys, values, prefix)


def scored_kernel(mixed, squares, gain, out, rows, sems):
    total = squares[0]
    for p in range(1, PEERS):
        total = total + squares[p]
    scale = lax.rsqrt(total / D + 1e-06)
    copies = []
    for t in range(mixed.shape[0] // HD):
        at = slice(t * HD, (t + 1) * HD)
        column = jnp.swapaxes(jnp.broadcast_to(scale[t : t + 1], (HD, HD)), 0, 1)
        for h in range(mixed.shape[1] // HD):
            cols = head_columns(h)
            rows[at, cols] = (mixed[at, cols] * column * gain[:, cols]).astype(jnp.bfloat16)
        part = pl.ds(t * HD, HD)
        copies.append(pltpu.make_async_copy(rows.at[part], out.at[part], sems.at[t]))
        copies[-1].start()
    for copy in copies:
        copy.wait()


def scored_part(mixed, squares, gain):
    rows, width = mixed.shape
    return pl.pallas_call(
        scored_kernel,
        in_specs=[VMEM] * 3,
        out_specs=HBM,
        out_shape=jax.ShapeDtypeStruct((rows, width), jnp.bfloat16),
        scratch_shapes=[pltpu.VMEM((rows, width), jnp.bfloat16), pltpu.SemaphoreType.DMA((rows // HD,))],
        compiler_params=grant(OTHER_MIB),
        name="scored",
    )(mixed, squares, gain.reshape(1, width))


def shards(queries, keys, values, gain):
    total = shard_state(keys, values)
    prefix = exclusive_states(total)
    mixed, squares = mixed_part(queries, keys, values, prefix)
    squares = lax.all_to_all(squares, "tp", 0, 0)
    return scored_part(mixed, squares, gain)


def solution(mesh):
    return jax.shard_map(
        shards,
        mesh=mesh,
        in_specs=(P("ctx", "tp"), P("ctx", "tp"), P("ctx", "tp"), P("tp")),
        out_specs=P("ctx", "tp"),
        check_vma=False,
    )
```

```python
import jax
import jax.numpy as jnp
from jax import lax
from jax.experimental import pallas as pl
from jax.experimental.pallas import tpu as pltpu
from jax.sharding import PartitionSpec as P

HD = 128
D = 4096
BLOCK = 512
XS = 4
ZS = 16
NEAR = 4
FAR = ZS // NEAR
MEMBERS = XS * NEAR
PEERS = 8
LOAD = 128
CHUNK = 256
STORE = 128
VMEM = pl.BlockSpec(memory_space=pltpu.VMEM)
HBM = pl.BlockSpec(memory_space=pltpu.HBM)
STATE_MIB = 53.2
MIXED_MIB = 32
OTHER_MIB = 32


def grant(mib):
    return pltpu.CompilerParams(vmem_limit_bytes=int(mib * 1024 * 1024))


def near_groups():
    return [[x * ZS + a * NEAR + b for x in range(XS) for b in range(NEAR)] for a in range(FAR)]


def between(pairs):
    return [(x * ZS + i * NEAR + b, x * ZS + j * NEAR + b) for x in range(XS) for b in range(NEAR) for i, j in pairs]


def contract_tokens(left, right):
    return lax.dot_general(left, right, (((0,), (0,)), ((), ())), preferred_element_type=jnp.float32)


def contract_last(left, right):
    return lax.dot_general(left, right, (((1,), (1,)), ((), ())), preferred_element_type=jnp.float32)


def head_columns(h):
    return slice(h * HD, (h + 1) * HD)


def state_kernel(keys, values, total, key_rows, value_rows, sems):
    rows, width = keys.shape
    parts = rows // LOAD
    copies = []
    for c in range(parts):
        at = pl.ds(c * LOAD, LOAD)
        pair = (
            pltpu.make_async_copy(keys.at[at], key_rows.at[at], sems.at[c]),
            pltpu.make_async_copy(values.at[at], value_rows.at[at], sems.at[parts + c]),
        )
        for copy in pair:
            copy.start()
        copies.append(pair)
    sums = [None] * (width // HD)
    for c in range(0, rows, CHUNK):
        for pair in copies[c // LOAD : (c + CHUNK) // LOAD]:
            for copy in pair:
                copy.wait()
        for h in range(len(sums)):
            cols = head_columns(h)
            part = contract_tokens(key_rows[c : c + CHUNK, cols], value_rows[c : c + CHUNK, cols])
            sums[h] = part if c == 0 else sums[h] + part
    for h, s in enumerate(sums):
        total[h] = s


def shard_state(keys, values):
    rows, width = keys.shape
    return pl.pallas_call(
        state_kernel,
        in_specs=[HBM, HBM],
        out_specs=VMEM,
        out_shape=jax.ShapeDtypeStruct((width // HD, HD, HD), jnp.float32),
        scratch_shapes=[
            pltpu.VMEM((rows, width), keys.dtype),
            pltpu.VMEM((rows, width), values.dtype),
            pltpu.SemaphoreType.DMA((2 * rows // LOAD,)),
        ],
        compiler_params=grant(STATE_MIB),
        cost_estimate=pl.CostEstimate(flops=2 * rows * width * HD, bytes_accessed=4 * rows * width, transcendentals=0),
        name="states",
    )(keys, values)


STEPS = (
    ((2, 0),),
    ((3, 0),),
    ((1, 0), (0, 1)),
    ((0, 3),),
    ((0, 2), (2, 1)),
    ((1, 3), (3, 1)),
    ((1, 2),),
    ((2, 3), (3, 2)),
)


def own_kernel(got, *outs):
    run = None
    for x in range(XS):
        for b in range(NEAR):
            run = got[x * NEAR + b] if run is None else run + got[x * NEAR + b]
        for out in outs:
            out[x] = run


def back_kernel(got, *rest):
    parts, back = rest[:-1], rest[-1]
    mine = (lax.axis_index("ctx") // NEAR) % FAR
    run = None
    for x in range(XS):
        start = jnp.zeros(got.shape[1:], jnp.float32) if run is None else run
        run = start
        for step, part in zip(STEPS, parts):
            shifted = [dst for src, dst in step if src > dst]
            if not shifted:
                start = start + part[x]
            elif len(shifted) == len(step):
                start = start + part[x - 1] if x else start
            else:
                moved = mine == shifted[0]
                for dst in shifted[1:]:
                    moved = moved | (mine == dst)
                before = part[x - 1] if x else jnp.zeros_like(start)
                start = start + jnp.where(moved, before, part[x])
        for b in range(NEAR):
            back[x * NEAR + b] = start
            if b < NEAR - 1:
                start = start + got[x * NEAR + b]
            run = run + got[x * NEAR + b]


def exclusive_states(state):
    rows = state.shape[0] * HD // MEMBERS
    pieces = state.reshape(MEMBERS, rows, HD)
    got = lax.all_to_all(pieces, "ctx", 0, 0, axis_index_groups=near_groups())
    sent = pl.pallas_call(
        own_kernel,
        in_specs=[VMEM],
        out_specs=[VMEM] * len(STEPS),
        out_shape=[jax.ShapeDtypeStruct((XS, rows, HD), jnp.float32)] * len(STEPS),
        compiler_params=grant(OTHER_MIB),
        name="sent",
    )(got)
    parts = [lax.ppermute(out, "ctx", between(step)) for out, step in zip(sent, STEPS)]
    back = pl.pallas_call(
        back_kernel,
        in_specs=[VMEM] * (1 + len(parts)),
        out_specs=VMEM,
        out_shape=jax.ShapeDtypeStruct(got.shape, jnp.float32),
        compiler_params=grant(OTHER_MIB),
        name="back",
    )(got, *parts)
    mine = lax.all_to_all(back, "ctx", 0, 0, axis_index_groups=near_groups())
    return mine.reshape(state.shape)


def mixed_kernel(queries, keys, values, prefix, mixed, squares):
    half = BLOCK // 2
    tiles = BLOCK // HD
    row = lax.broadcasted_iota(jnp.int32, (half, half), 0)
    col = lax.broadcasted_iota(jnp.int32, (half, half), 1)
    lower = row >= col
    for start in range(0, queries.shape[0], BLOCK):
        top_rows = slice(start, start + half)
        low_rows = slice(start + half, start + BLOCK)
        acc = [None, None]
        for h in range(queries.shape[1] // HD):
            cols = head_columns(h)
            state = prefix[h]
            if start:
                state = state + contract_tokens(keys[:start, cols], values[:start, cols])
            state = state.astype(jnp.bfloat16)
            q, k = queries[top_rows, cols], keys[top_rows, cols]
            top = jnp.where(lower, contract_last(q, k), 0.0).astype(jnp.bfloat16)
            m = jnp.dot(q, state, preferred_element_type=jnp.float32)
            m = m + jnp.dot(top, values[top_rows, cols], preferred_element_type=jnp.float32)
            mixed[top_rows, cols] = m
            acc[0] = m * m if h == 0 else acc[0] + m * m
            q = queries[low_rows, cols]
            side = contract_last(q, k).astype(jnp.bfloat16)
            low = jnp.where(lower, contract_last(q, keys[low_rows, cols]), 0.0).astype(jnp.bfloat16)
            both = jnp.concatenate([side, low], axis=1)
            m = jnp.dot(q, state, preferred_element_type=jnp.float32)
            m = m + jnp.dot(both, values[start : start + BLOCK, cols], preferred_element_type=jnp.float32)
            mixed[low_rows, cols] = m
            acc[1] = m * m if h == 0 else acc[1] + m * m
        for i, a in enumerate(acc):
            turned = jnp.swapaxes(a.reshape(tiles // 2, HD, HD), 1, 2)
            sums = jnp.sum(turned, axis=1)
            at = start // HD + i * (tiles // 2)
            for p in range(PEERS):
                squares[p, at : at + tiles // 2] = sums


def mixed_part(queries, keys, values, prefix):
    rows, width = queries.shape
    return pl.pallas_call(
        mixed_kernel,
        in_specs=[VMEM] * 4,
        out_specs=[VMEM] * 2,
        out_shape=[
            jax.ShapeDtypeStruct((rows, width), jnp.float32),
            jax.ShapeDtypeStruct((PEERS, rows // HD, HD), jnp.float32),
        ],
        compiler_params=grant(MIXED_MIB),
        cost_estimate=pl.CostEstimate(flops=4 * rows * BLOCK * width, bytes_accessed=10 * rows * width, transcendentals=0),
        name="mixed",
    )(queries, keys, values, prefix)


def scored_kernel(mixed, squares, gain, out, rows, sems):
    total = squares[0]
    for p in range(1, PEERS):
        total = total + squares[p]
    scale = lax.rsqrt(total / D + 1e-06)
    copies = []
    for t in range(mixed.shape[0] // HD):
        at = slice(t * HD, (t + 1) * HD)
        column = jnp.swapaxes(jnp.broadcast_to(scale[t : t + 1], (HD, HD)), 0, 1)
        for h in range(mixed.shape[1] // HD):
            cols = head_columns(h)
            rows[at, cols] = (mixed[at, cols] * column * gain[:, cols]).astype(jnp.bfloat16)
        part = pl.ds(t * HD, HD)
        copies.append(pltpu.make_async_copy(rows.at[part], out.at[part], sems.at[t]))
        copies[-1].start()
    for copy in copies:
        copy.wait()


def scored_part(mixed, squares, gain):
    rows, width = mixed.shape
    return pl.pallas_call(
        scored_kernel,
        in_specs=[VMEM] * 3,
        out_specs=HBM,
        out_shape=jax.ShapeDtypeStruct((rows, width), jnp.bfloat16),
        scratch_shapes=[pltpu.VMEM((rows, width), jnp.bfloat16), pltpu.SemaphoreType.DMA((rows // HD,))],
        compiler_params=grant(OTHER_MIB),
        name="scored",
    )(mixed, squares, gain.reshape(1, width))


def shards(queries, keys, values, gain):
    total = shard_state(keys, values)
    prefix = exclusive_states(total)
    mixed, squares = mixed_part(queries, keys, values, prefix)
    squares = lax.all_to_all(squares, "tp", 0, 0)
    return scored_part(mixed, squares, gain)


def solution(mesh):
    return jax.shard_map(
        shards,
        mesh=mesh,
        in_specs=(P("ctx", "tp"), P("ctx", "tp"), P("ctx", "tp"), P("tp")),
        out_specs=P("ctx", "tp"),
        check_vma=False,
    )
```

```python
import jax
import jax.numpy as jnp
from jax import lax
from jax.experimental import pallas as pl
from jax.experimental.pallas import tpu as pltpu
from jax.sharding import PartitionSpec as P

HD = 128
D = 4096
BLOCK = 512
XS = 4
ZS = 16
NEAR = 4
FAR = ZS // NEAR
MEMBERS = XS * NEAR
PEERS = 8
LOAD = 128
CHUNK = 256
STORE = 128
VMEM = pl.BlockSpec(memory_space=pltpu.VMEM)
HBM = pl.BlockSpec(memory_space=pltpu.HBM)
STATE_MIB = 53.2
LOCAL_MIB = 32
MIXED_MIB = 32
OTHER_MIB = 32


def grant(mib):
    return pltpu.CompilerParams(vmem_limit_bytes=int(mib * 1024 * 1024))


def near_groups():
    return [[x * ZS + a * NEAR + b for x in range(XS) for b in range(NEAR)] for a in range(FAR)]


def between(pairs):
    return [(x * ZS + i * NEAR + b, x * ZS + j * NEAR + b) for x in range(XS) for b in range(NEAR) for i, j in pairs]


def contract_tokens(left, right):
    return lax.dot_general(left, right, (((0,), (0,)), ((), ())), preferred_element_type=jnp.float32)


def contract_last(left, right):
    return lax.dot_general(left, right, (((1,), (1,)), ((), ())), preferred_element_type=jnp.float32)


def head_columns(h):
    return slice(h * HD, (h + 1) * HD)


def state_kernel(keys, values, total, key_rows, value_rows, sems):
    rows, width = keys.shape
    parts = rows // LOAD
    copies = []
    for c in range(parts):
        at = pl.ds(c * LOAD, LOAD)
        pair = (
            pltpu.make_async_copy(keys.at[at], key_rows.at[at], sems.at[c]),
            pltpu.make_async_copy(values.at[at], value_rows.at[at], sems.at[parts + c]),
        )
        for copy in pair:
            copy.start()
        copies.append(pair)
    sums = [None] * (width // HD)
    for c in range(0, rows, CHUNK):
        for pair in copies[c // LOAD : (c + CHUNK) // LOAD]:
            for copy in pair:
                copy.wait()
        for h in range(len(sums)):
            cols = head_columns(h)
            part = contract_tokens(key_rows[c : c + CHUNK, cols], value_rows[c : c + CHUNK, cols])
            sums[h] = part if c == 0 else sums[h] + part
    for h, s in enumerate(sums):
        total[h] = s


def shard_state(keys, values):
    rows, width = keys.shape
    return pl.pallas_call(
        state_kernel,
        in_specs=[HBM, HBM],
        out_specs=VMEM,
        out_shape=jax.ShapeDtypeStruct((width // HD, HD, HD), jnp.float32),
        scratch_shapes=[
            pltpu.VMEM((rows, width), keys.dtype),
            pltpu.VMEM((rows, width), values.dtype),
            pltpu.SemaphoreType.DMA((2 * rows // LOAD,)),
        ],
        compiler_params=grant(STATE_MIB),
        cost_estimate=pl.CostEstimate(flops=2 * rows * width * HD, bytes_accessed=4 * rows * width, transcendentals=0),
        name="states",
    )(keys, values)


STEPS = (
    ((2, 0),),
    ((3, 0),),
    ((1, 0), (0, 1)),
    ((0, 3),),
    ((0, 2), (2, 1)),
    ((1, 3), (3, 1)),
    ((1, 2),),
    ((2, 3), (3, 2)),
)


def own_kernel(got, *outs):
    run = None
    for x in range(XS):
        for b in range(NEAR):
            run = got[x * NEAR + b] if run is None else run + got[x * NEAR + b]
        for out in outs:
            out[x] = run


def back_kernel(meanwhile, got, *rest):
    parts, back = rest[:-1], rest[-1]
    mine = (lax.axis_index("ctx") // NEAR) % FAR
    run = None
    for x in range(XS):
        start = jnp.zeros(got.shape[1:], jnp.float32) if run is None else run
        run = start
        for step, part in zip(STEPS, parts):
            shifted = [dst for src, dst in step if src > dst]
            if not shifted:
                start = start + part[x]
            elif len(shifted) == len(step):
                start = start + part[x - 1] if x else start
            else:
                moved = mine == shifted[0]
                for dst in shifted[1:]:
                    moved = moved | (mine == dst)
                before = part[x - 1] if x else jnp.zeros_like(start)
                start = start + jnp.where(moved, before, part[x])
        for b in range(NEAR):
            back[x * NEAR + b] = start
            if b < NEAR - 1:
                start = start + got[x * NEAR + b]
            run = run + got[x * NEAR + b]


def exclusive_states(state, meanwhile):
    rows = state.shape[0] * HD // MEMBERS
    pieces = state.reshape(MEMBERS, rows, HD)
    got = lax.all_to_all(pieces, "ctx", 0, 0, axis_index_groups=near_groups())
    sent = pl.pallas_call(
        own_kernel,
        in_specs=[VMEM],
        out_specs=[VMEM] * len(STEPS),
        out_shape=[jax.ShapeDtypeStruct((XS, rows, HD), jnp.float32)] * len(STEPS),
        compiler_params=grant(OTHER_MIB),
        name="sent",
    )(got)
    parts = [lax.ppermute(out, "ctx", between(step)) for out, step in zip(sent, STEPS)]
    back = pl.pallas_call(
        back_kernel,
        in_specs=[HBM] + [VMEM] * (1 + len(parts)),
        out_specs=VMEM,
        out_shape=jax.ShapeDtypeStruct(got.shape, jnp.float32),
        compiler_params=grant(OTHER_MIB),
        name="back",
    )(meanwhile, got, *parts)
    mine = lax.all_to_all(back, "ctx", 0, 0, axis_index_groups=near_groups())
    return mine.reshape(state.shape)


def local_kernel(queries, keys, values, out, first, top_queries):
    half = BLOCK // 2
    row = lax.broadcasted_iota(jnp.int32, (half, half), 0)
    col = lax.broadcasted_iota(jnp.int32, (half, half), 1)
    lower = row >= col
    top_queries[...] = queries[:BLOCK]
    for h in range(queries.shape[1] // HD):
        cols = head_columns(h)
        first[h] = contract_tokens(keys[:BLOCK, cols], values[:BLOCK, cols])
        for start in range(0, queries.shape[0], BLOCK):
            top_rows = slice(start, start + half)
            low_rows = slice(start + half, start + BLOCK)
            q, k = queries[top_rows, cols], keys[top_rows, cols]
            top = jnp.where(lower, contract_last(q, k), 0.0).astype(jnp.bfloat16)
            out[top_rows, cols] = jnp.dot(top, values[top_rows, cols], preferred_element_type=jnp.float32)
            q = queries[low_rows, cols]
            side = contract_last(q, k).astype(jnp.bfloat16)
            low = jnp.where(lower, contract_last(q, keys[low_rows, cols]), 0.0).astype(jnp.bfloat16)
            both = jnp.concatenate([side, low], axis=1)
            v = values[start : start + BLOCK, cols]
            out[low_rows, cols] = jnp.dot(both, v, preferred_element_type=jnp.float32)


def local_part(queries, keys, values):
    rows, width = queries.shape
    return pl.pallas_call(
        local_kernel,
        in_specs=[VMEM] * 3,
        out_specs=[VMEM] * 3,
        out_shape=[
            jax.ShapeDtypeStruct((rows, width), jnp.float32),
            jax.ShapeDtypeStruct((width // HD, HD, HD), jnp.float32),
            jax.ShapeDtypeStruct((BLOCK, width), queries.dtype),
        ],
        compiler_params=grant(LOCAL_MIB),
        cost_estimate=pl.CostEstimate(flops=4 * rows * BLOCK * width, bytes_accessed=10 * rows * width, transcendentals=0),
        name="local",
    )(queries, keys, values)


def mixed_kernel(queries, top_queries, local, prefix, first, mixed, squares, held, sem):
    tiles = BLOCK // HD
    rest = pltpu.make_async_copy(queries.at[pl.ds(BLOCK, BLOCK)], held, sem)
    rest.start()
    for i in range(local.shape[0] // BLOCK):
        if i:
            rest.wait()
        rows = slice(i * BLOCK, (i + 1) * BLOCK)
        acc = None
        for h in range(local.shape[1] // HD):
            cols = head_columns(h)
            state = prefix[h] + first[h] if i else prefix[h]
            q = held[:, cols] if i else top_queries[:, cols]
            m = jnp.dot(q, state.astype(jnp.bfloat16), preferred_element_type=jnp.float32) + local[rows, cols]
            mixed[rows, cols] = m
            acc = m * m if h == 0 else acc + m * m
        turned = jnp.swapaxes(acc.reshape(tiles, HD, HD), 1, 2)
        sums = jnp.sum(turned, axis=1)
        for p in range(PEERS):
            squares[p, i * tiles : (i + 1) * tiles] = sums


def mixed_part(queries, top_queries, local, prefix, first):
    rows, width = queries.shape
    return pl.pallas_call(
        mixed_kernel,
        in_specs=[HBM] + [VMEM] * 4,
        out_specs=[VMEM] * 2,
        out_shape=[
            jax.ShapeDtypeStruct((rows, width), jnp.float32),
            jax.ShapeDtypeStruct((PEERS, rows // HD, HD), jnp.float32),
        ],
        scratch_shapes=[pltpu.VMEM((BLOCK, width), queries.dtype), pltpu.SemaphoreType.DMA(())],
        compiler_params=grant(MIXED_MIB),
        cost_estimate=pl.CostEstimate(flops=2 * rows * HD * width, bytes_accessed=10 * rows * width, transcendentals=0),
        name="mixed",
    )(queries, top_queries, local, prefix, first)


def scored_kernel(mixed, squares, gain, out, rows, sems):
    total = squares[0]
    for p in range(1, PEERS):
        total = total + squares[p]
    scale = lax.rsqrt(total / D + 1e-06)
    copies = []
    for t in range(mixed.shape[0] // HD):
        at = slice(t * HD, (t + 1) * HD)
        column = jnp.swapaxes(jnp.broadcast_to(scale[t : t + 1], (HD, HD)), 0, 1)
        for h in range(mixed.shape[1] // HD):
            cols = head_columns(h)
            rows[at, cols] = (mixed[at, cols] * column * gain[:, cols]).astype(jnp.bfloat16)
        part = pl.ds(t * HD, HD)
        copies.append(pltpu.make_async_copy(rows.at[part], out.at[part], sems.at[t]))
        copies[-1].start()
    for copy in copies:
        copy.wait()


def scored_part(mixed, squares, gain):
    rows, width = mixed.shape
    return pl.pallas_call(
        scored_kernel,
        in_specs=[VMEM] * 3,
        out_specs=HBM,
        out_shape=jax.ShapeDtypeStruct((rows, width), jnp.bfloat16),
        scratch_shapes=[pltpu.VMEM((rows, width), jnp.bfloat16), pltpu.SemaphoreType.DMA((rows // HD,))],
        compiler_params=grant(OTHER_MIB),
        name="scored",
    )(mixed, squares, gain.reshape(1, width))


def shards(queries, keys, values, gain):
    total = shard_state(keys, values)
    local, first, top_queries = local_part(queries, keys, values)
    prefix = exclusive_states(total, first)
    mixed, squares = mixed_part(queries, top_queries, local, prefix, first)
    squares = lax.all_to_all(squares, "tp", 0, 0)
    return scored_part(mixed, squares, gain)


def solution(mesh):
    return jax.shard_map(
        shards,
        mesh=mesh,
        in_specs=(P("ctx", "tp"), P("ctx", "tp"), P("ctx", "tp"), P("tp")),
        out_specs=P("ctx", "tp"),
        check_vma=False,
    )
```

```python
import functools

import jax
import jax.numpy as jnp
from jax import lax
from jax.experimental import pallas as pl
from jax.experimental.pallas import tpu as pltpu
from jax.sharding import PartitionSpec as P

HD = 128
D = 4096
BLOCK = 512
XS = 4
ZS = 16
NEAR = 4
FAR = ZS // NEAR
MEMBERS = XS * NEAR
PEERS = 8
LOAD = 128
CHUNK = 256
STORE = 128
VMEM = pl.BlockSpec(memory_space=pltpu.VMEM)
HBM = pl.BlockSpec(memory_space=pltpu.HBM)
STATE_MIB = 53.2
LOCAL_MIB = 32
EARLY = 1
MIXED_MIB = 32
OTHER_MIB = 32


def grant(mib):
    return pltpu.CompilerParams(vmem_limit_bytes=int(mib * 1024 * 1024))


def near_groups():
    return [[x * ZS + a * NEAR + b for x in range(XS) for b in range(NEAR)] for a in range(FAR)]


def between(pairs):
    return [(x * ZS + i * NEAR + b, x * ZS + j * NEAR + b) for x in range(XS) for b in range(NEAR) for i, j in pairs]


def contract_tokens(left, right):
    return lax.dot_general(left, right, (((0,), (0,)), ((), ())), preferred_element_type=jnp.float32)


def contract_last(left, right):
    return lax.dot_general(left, right, (((1,), (1,)), ((), ())), preferred_element_type=jnp.float32)


def head_columns(h):
    return slice(h * HD, (h + 1) * HD)


def state_kernel(keys, values, total, key_rows, value_rows, sems):
    rows, width = keys.shape
    parts = rows // LOAD
    copies = []
    for c in range(parts):
        at = pl.ds(c * LOAD, LOAD)
        pair = (
            pltpu.make_async_copy(keys.at[at], key_rows.at[at], sems.at[c]),
            pltpu.make_async_copy(values.at[at], value_rows.at[at], sems.at[parts + c]),
        )
        for copy in pair:
            copy.start()
        copies.append(pair)
    sums = [None] * (width // HD)
    for c in range(0, rows, CHUNK):
        for pair in copies[c // LOAD : (c + CHUNK) // LOAD]:
            for copy in pair:
                copy.wait()
        for h in range(len(sums)):
            cols = head_columns(h)
            part = contract_tokens(key_rows[c : c + CHUNK, cols], value_rows[c : c + CHUNK, cols])
            sums[h] = part if c == 0 else sums[h] + part
    for h, s in enumerate(sums):
        total[h] = s


def shard_state(keys, values):
    rows, width = keys.shape
    return pl.pallas_call(
        state_kernel,
        in_specs=[HBM, HBM],
        out_specs=VMEM,
        out_shape=jax.ShapeDtypeStruct((width // HD, HD, HD), jnp.float32),
        scratch_shapes=[
            pltpu.VMEM((rows, width), keys.dtype),
            pltpu.VMEM((rows, width), values.dtype),
            pltpu.SemaphoreType.DMA((2 * rows // LOAD,)),
        ],
        compiler_params=grant(STATE_MIB),
        cost_estimate=pl.CostEstimate(flops=2 * rows * width * HD, bytes_accessed=4 * rows * width, transcendentals=0),
        name="states",
    )(keys, values)


STEPS = (
    ((2, 0),),
    ((1, 0), (2, 1),),
    ((3, 0), (0, 3),),
    ((0, 1), (2, 3),),
    ((3, 1), (1, 3),),
    ((1, 2),),
    ((3, 2),),
)
RELAY = len(STEPS) - 1
CARRIED = 2
WITH = (0, 1)
LOCAL_AFTER = 1


def relay_kernel(own, *rest):
    carried, out = rest[len(WITH)], rest[-1]
    src, dst = STEPS[RELAY][0]
    for x in range(XS):
        if src < dst:
            out[x] = own[x] + carried[x]
        else:
            out[x] = own[x - 1] + carried[x] if x else carried[x]


def own_kernel(got, *outs):
    run = None
    for x in range(XS):
        for b in range(NEAR):
            run = got[x * NEAR + b] if run is None else run + got[x * NEAR + b]
        for out in outs:
            out[x] = run


def back_kernel(meanwhile, got, *rest):
    parts, back = rest[:-1], rest[-1]
    mine = (lax.axis_index("ctx") // NEAR) % FAR
    run = None
    for x in range(XS):
        start = jnp.zeros(got.shape[1:], jnp.float32) if run is None else run
        run = start
        for k, (step, part) in enumerate(zip(STEPS, parts)):
            shifted = [dst for src, dst in step if src > dst and k != RELAY]
            if not shifted:
                start = start + part[x]
            elif len(shifted) == len(step):
                start = start + part[x - 1] if x else start
            else:
                moved = mine == shifted[0]
                for dst in shifted[1:]:
                    moved = moved | (mine == dst)
                before = part[x - 1] if x else jnp.zeros_like(start)
                start = start + jnp.where(moved, before, part[x])
        for b in range(NEAR):
            back[x * NEAR + b] = start
            if b < NEAR - 1:
                start = start + got[x * NEAR + b]
            run = run + got[x * NEAR + b]


def exclusive_states(state, local):
    rows = state.shape[0] * HD // MEMBERS
    pieces = state.reshape(MEMBERS, rows, HD)
    got = lax.all_to_all(pieces, "ctx", 0, 0, axis_index_groups=near_groups())
    sent = pl.pallas_call(
        own_kernel,
        in_specs=[VMEM],
        out_specs=[VMEM] * len(STEPS),
        out_shape=[jax.ShapeDtypeStruct((XS, rows, HD), jnp.float32)] * len(STEPS),
        compiler_params=grant(OTHER_MIB),
        name="sent",
    )(got)
    parts = []
    for k, step in enumerate(STEPS):
        out = sent[k]
        if k == RELAY:
            held = local(parts[LOCAL_AFTER])
            late = [parts[j] for j in (*WITH, CARRIED)] + [held[1]]
            out = pl.pallas_call(
                relay_kernel,
                in_specs=[VMEM] * len(late) + [HBM],
                out_specs=VMEM,
                out_shape=jax.ShapeDtypeStruct(out.shape, jnp.float32),
                compiler_params=grant(OTHER_MIB),
                name="relay",
            )(out, *late)
        parts.append(lax.ppermute(out, "ctx", between(step)))
    held = local(out, held)
    back = pl.pallas_call(
        back_kernel,
        in_specs=[HBM] + [VMEM] * (1 + len(parts)),
        out_specs=VMEM,
        out_shape=jax.ShapeDtypeStruct(got.shape, jnp.float32),
        compiler_params=grant(OTHER_MIB),
        name="back",
    )(held[1], got, *parts)
    mine = lax.all_to_all(back, "ctx", 0, 0, axis_index_groups=near_groups())
    return mine.reshape(state.shape), held


def local_kernel(early, queries, keys, values, *rest):
    out, first, top_queries = rest[-3:]
    leading = (lax.axis_index("ctx") // NEAR) % FAR < EARLY

    @pl.when(leading == early)
    def _():
        local_work(queries, keys, values, out, first, top_queries)


def local_work(queries, keys, values, out, first, top_queries):
    half = BLOCK // 2
    row = lax.broadcasted_iota(jnp.int32, (half, half), 0)
    col = lax.broadcasted_iota(jnp.int32, (half, half), 1)
    lower = row >= col
    top_queries[...] = queries[:BLOCK]
    for h in range(queries.shape[1] // HD):
        cols = head_columns(h)
        first[h] = contract_tokens(keys[:BLOCK, cols], values[:BLOCK, cols])
        for start in range(0, queries.shape[0], BLOCK):
            top_rows = slice(start, start + half)
            low_rows = slice(start + half, start + BLOCK)
            q, k = queries[top_rows, cols], keys[top_rows, cols]
            top = jnp.where(lower, contract_last(q, k), 0.0).astype(jnp.bfloat16)
            out[top_rows, cols] = jnp.dot(top, values[top_rows, cols], preferred_element_type=jnp.float32)
            q = queries[low_rows, cols]
            side = contract_last(q, k).astype(jnp.bfloat16)
            low = jnp.where(lower, contract_last(q, keys[low_rows, cols]), 0.0).astype(jnp.bfloat16)
            both = jnp.concatenate([side, low], axis=1)
            v = values[start : start + BLOCK, cols]
            out[low_rows, cols] = jnp.dot(both, v, preferred_element_type=jnp.float32)


def local_part(queries, keys, values, after, held=None):
    rows, width = queries.shape
    more = [after] + (list(held) if held else [])
    return pl.pallas_call(
        functools.partial(local_kernel, held is None),
        in_specs=[VMEM] * 3 + [HBM] + [VMEM] * (len(more) - 1),
        out_specs=[VMEM] * 3,
        out_shape=[
            jax.ShapeDtypeStruct((rows, width), jnp.float32),
            jax.ShapeDtypeStruct((width // HD, HD, HD), jnp.float32),
            jax.ShapeDtypeStruct((BLOCK, width), queries.dtype),
        ],
        input_output_aliases={4 + i: i for i in range(3)} if held else {},
        compiler_params=grant(LOCAL_MIB),
        cost_estimate=pl.CostEstimate(flops=4 * rows * BLOCK * width, bytes_accessed=10 * rows * width, transcendentals=0),
        name="local",
    )(queries, keys, values, *more)


def mixed_kernel(queries, top_queries, local, prefix, first, mixed, squares, held, sem):
    tiles = BLOCK // HD
    rest = pltpu.make_async_copy(queries.at[pl.ds(BLOCK, BLOCK)], held, sem)
    rest.start()
    for i in range(local.shape[0] // BLOCK):
        if i:
            rest.wait()
        rows = slice(i * BLOCK, (i + 1) * BLOCK)
        acc = None
        for h in range(local.shape[1] // HD):
            cols = head_columns(h)
            state = prefix[h] + first[h] if i else prefix[h]
            q = held[:, cols] if i else top_queries[:, cols]
            m = jnp.dot(q, state.astype(jnp.bfloat16), preferred_element_type=jnp.float32) + local[rows, cols]
            mixed[rows, cols] = m
            acc = m * m if h == 0 else acc + m * m
        turned = jnp.swapaxes(acc.reshape(tiles, HD, HD), 1, 2)
        sums = jnp.sum(turned, axis=1)
        for p in range(PEERS):
            squares[p, i * tiles : (i + 1) * tiles] = sums


def mixed_part(queries, top_queries, local, prefix, first):
    rows, width = queries.shape
    return pl.pallas_call(
        mixed_kernel,
        in_specs=[HBM] + [VMEM] * 4,
        out_specs=[VMEM] * 2,
        out_shape=[
            jax.ShapeDtypeStruct((rows, width), jnp.float32),
            jax.ShapeDtypeStruct((PEERS, rows // HD, HD), jnp.float32),
        ],
        scratch_shapes=[pltpu.VMEM((BLOCK, width), queries.dtype), pltpu.SemaphoreType.DMA(())],
        compiler_params=grant(MIXED_MIB),
        cost_estimate=pl.CostEstimate(flops=2 * rows * HD * width, bytes_accessed=10 * rows * width, transcendentals=0),
        name="mixed",
    )(queries, top_queries, local, prefix, first)


def scored_kernel(mixed, squares, gain, out, rows, sems):
    total = squares[0]
    for p in range(1, PEERS):
        total = total + squares[p]
    scale = lax.rsqrt(total / D + 1e-06)
    copies = []
    for t in range(mixed.shape[0] // HD):
        at = slice(t * HD, (t + 1) * HD)
        column = jnp.swapaxes(jnp.broadcast_to(scale[t : t + 1], (HD, HD)), 0, 1)
        for h in range(mixed.shape[1] // HD):
            cols = head_columns(h)
            rows[at, cols] = (mixed[at, cols] * column * gain[:, cols]).astype(jnp.bfloat16)
        part = pl.ds(t * HD, HD)
        copies.append(pltpu.make_async_copy(rows.at[part], out.at[part], sems.at[t]))
        copies[-1].start()
    for copy in copies:
        copy.wait()


def scored_part(mixed, squares, gain):
    rows, width = mixed.shape
    return pl.pallas_call(
        scored_kernel,
        in_specs=[VMEM] * 3,
        out_specs=HBM,
        out_shape=jax.ShapeDtypeStruct((rows, width), jnp.bfloat16),
        scratch_shapes=[pltpu.VMEM((rows, width), jnp.bfloat16), pltpu.SemaphoreType.DMA((rows // HD,))],
        compiler_params=grant(OTHER_MIB),
        name="scored",
    )(mixed, squares, gain.reshape(1, width))


def shards(queries, keys, values, gain):
    total = shard_state(keys, values)
    prefix, (local, first, top_queries) = exclusive_states(total, functools.partial(local_part, queries, keys, values))
    mixed, squares = mixed_part(queries, top_queries, local, prefix, first)
    squares = lax.all_to_all(squares, "tp", 0, 0)
    return scored_part(mixed, squares, gain)


def solution(mesh):
    return jax.shard_map(
        shards,
        mesh=mesh,
        in_specs=(P("ctx", "tp"), P("ctx", "tp"), P("ctx", "tp"), P("tp")),
        out_specs=P("ctx", "tp"),
        check_vma=False,
    )
```

```python
import functools

import jax
import jax.numpy as jnp
from jax import lax
from jax.experimental import pallas as pl
from jax.experimental.pallas import tpu as pltpu
from jax.sharding import PartitionSpec as P

HD = 128
D = 4096
BLOCK = 512
XS = 4
ZS = 16
NEAR = 4
FAR = ZS // NEAR
MEMBERS = XS * NEAR
PEERS = 8
LOAD = 128
CHUNK = 256
STORE = 128
VMEM = pl.BlockSpec(memory_space=pltpu.VMEM)
HBM = pl.BlockSpec(memory_space=pltpu.HBM)
STATE_MIB = 53.2
LOCAL_MIB = 32
EARLY = 1
MIXED_MIB = 32
OTHER_MIB = 32


def grant(mib):
    return pltpu.CompilerParams(vmem_limit_bytes=int(mib * 1024 * 1024))


def near_groups():
    return [[x * ZS + a * NEAR + b for x in range(XS) for b in range(NEAR)] for a in range(FAR)]


def between(pairs):
    return [(x * ZS + i * NEAR + b, x * ZS + j * NEAR + b) for x in range(XS) for b in range(NEAR) for i, j in pairs]


def contract_tokens(left, right):
    return lax.dot_general(left, right, (((0,), (0,)), ((), ())), preferred_element_type=jnp.float32)


def contract_last(left, right):
    return lax.dot_general(left, right, (((1,), (1,)), ((), ())), preferred_element_type=jnp.float32)


def head_columns(h):
    return slice(h * HD, (h + 1) * HD)


def state_kernel(keys, values, total, key_rows, value_rows, sems):
    rows, width = keys.shape
    parts = rows // LOAD
    copies = []
    for c in range(parts):
        at = pl.ds(c * LOAD, LOAD)
        pair = (
            pltpu.make_async_copy(keys.at[at], key_rows.at[at], sems.at[c]),
            pltpu.make_async_copy(values.at[at], value_rows.at[at], sems.at[parts + c]),
        )
        for copy in pair:
            copy.start()
        copies.append(pair)
    sums = [None] * (width // HD)
    for c in range(0, rows, CHUNK):
        for pair in copies[c // LOAD : (c + CHUNK) // LOAD]:
            for copy in pair:
                copy.wait()
        for h in range(len(sums)):
            cols = head_columns(h)
            part = contract_tokens(key_rows[c : c + CHUNK, cols], value_rows[c : c + CHUNK, cols])
            sums[h] = part if c == 0 else sums[h] + part
    for h, s in enumerate(sums):
        total[h] = s


def shard_state(keys, values):
    rows, width = keys.shape
    return pl.pallas_call(
        state_kernel,
        in_specs=[HBM, HBM],
        out_specs=VMEM,
        out_shape=jax.ShapeDtypeStruct((width // HD, HD, HD), jnp.float32),
        scratch_shapes=[
            pltpu.VMEM((rows, width), keys.dtype),
            pltpu.VMEM((rows, width), values.dtype),
            pltpu.SemaphoreType.DMA((2 * rows // LOAD,)),
        ],
        compiler_params=grant(STATE_MIB),
        cost_estimate=pl.CostEstimate(flops=2 * rows * width * HD, bytes_accessed=4 * rows * width, transcendentals=0),
        name="states",
    )(keys, values)


STEPS = (
    ((2, 0),),
    ((2, 1), (3, 0),),
    ((0, 3), (1, 0),),
    ((0, 1), (2, 3),),
    ((1, 3), (3, 1),),
    ((1, 2),),
    ((3, 2),),
)
RELAY = len(STEPS) - 1
CARRIED = 2
WITH = (1, 0)
LOCAL_AFTER = 0


def relay_kernel(own, *rest):
    carried, out = rest[len(WITH)], rest[-1]
    src, dst = STEPS[RELAY][0]
    for x in range(XS):
        if src < dst:
            out[x] = own[x] + carried[x]
        else:
            out[x] = own[x - 1] + carried[x] if x else carried[x]


def rows_sent(step):
    return XS if any(src < dst for src, dst in STEPS[step]) or step == RELAY else XS - 1


def own_kernel(got, *outs):
    run = None
    for x in range(XS):
        for b in range(NEAR):
            run = got[x * NEAR + b] if run is None else run + got[x * NEAR + b]
        for out in outs:
            if x < out.shape[0]:
                out[x] = run


def back_kernel(meanwhile, got, *rest):
    parts, back = rest[:-1], rest[-1]
    mine = (lax.axis_index("ctx") // NEAR) % FAR
    run = None
    for x in range(XS):
        start = jnp.zeros(got.shape[1:], jnp.float32) if run is None else run
        run = start
        for k, (step, part) in enumerate(zip(STEPS, parts)):
            shifted = [dst for src, dst in step if src > dst and k != RELAY]
            if not shifted:
                start = start + part[x]
            elif len(shifted) == len(step):
                start = start + part[x - 1] if x else start
            else:
                moved = mine == shifted[0]
                for dst in shifted[1:]:
                    moved = moved | (mine == dst)
                before = part[x - 1] if x else jnp.zeros_like(start)
                start = start + jnp.where(moved, before, part[x])
        for b in range(NEAR):
            back[x * NEAR + b] = start
            if b < NEAR - 1:
                start = start + got[x * NEAR + b]
            run = run + got[x * NEAR + b]


def exclusive_states(state, local):
    rows = state.shape[0] * HD // MEMBERS
    pieces = state.reshape(MEMBERS, rows, HD)
    got = lax.all_to_all(pieces, "ctx", 0, 0, axis_index_groups=near_groups())
    sent = pl.pallas_call(
        own_kernel,
        in_specs=[VMEM],
        out_specs=[VMEM] * len(STEPS),
        out_shape=[jax.ShapeDtypeStruct((rows_sent(k), rows, HD), jnp.float32) for k in range(len(STEPS))],
        compiler_params=grant(OTHER_MIB),
        name="sent",
    )(got)
    parts = []
    for k, step in enumerate(STEPS):
        out = sent[k]
        if k == RELAY:
            held = local(sent[0])
            late = [parts[j] for j in (*WITH, CARRIED)] + [held[1]]
            out = pl.pallas_call(
                relay_kernel,
                in_specs=[VMEM] * len(late) + [HBM],
                out_specs=VMEM,
                out_shape=jax.ShapeDtypeStruct(out.shape, jnp.float32),
                compiler_params=grant(OTHER_MIB),
                name="relay",
            )(out, *late)
        parts.append(lax.ppermute(out, "ctx", between(step)))
    held = local(out, held)
    back = pl.pallas_call(
        back_kernel,
        in_specs=[HBM] + [VMEM] * (1 + len(parts)),
        out_specs=VMEM,
        out_shape=jax.ShapeDtypeStruct(got.shape, jnp.float32),
        compiler_params=grant(OTHER_MIB),
        name="back",
    )(held[1], got, *parts)
    mine = lax.all_to_all(back, "ctx", 0, 0, axis_index_groups=near_groups())
    return mine.reshape(state.shape), held


def local_kernel(early, queries, keys, values, *rest):
    out, first, top_queries = rest[-3:]
    leading = (lax.axis_index("ctx") // NEAR) % FAR < EARLY

    @pl.when(leading == early)
    def _():
        local_work(queries, keys, values, out, first, top_queries)


def local_work(queries, keys, values, out, first, top_queries):
    half = BLOCK // 2
    row = lax.broadcasted_iota(jnp.int32, (half, half), 0)
    col = lax.broadcasted_iota(jnp.int32, (half, half), 1)
    lower = row >= col
    top_queries[...] = queries[:BLOCK]
    for h in range(queries.shape[1] // HD):
        cols = head_columns(h)
        first[h] = contract_tokens(keys[:BLOCK, cols], values[:BLOCK, cols])
        for start in range(0, queries.shape[0], BLOCK):
            top_rows = slice(start, start + half)
            low_rows = slice(start + half, start + BLOCK)
            q, k = queries[top_rows, cols], keys[top_rows, cols]
            top = jnp.where(lower, contract_last(q, k), 0.0).astype(jnp.bfloat16)
            out[top_rows, cols] = jnp.dot(top, values[top_rows, cols], preferred_element_type=jnp.float32)
            q = queries[low_rows, cols]
            side = contract_last(q, k).astype(jnp.bfloat16)
            low = jnp.where(lower, contract_last(q, keys[low_rows, cols]), 0.0).astype(jnp.bfloat16)
            both = jnp.concatenate([side, low], axis=1)
            v = values[start : start + BLOCK, cols]
            out[low_rows, cols] = jnp.dot(both, v, preferred_element_type=jnp.float32)


def local_part(queries, keys, values, after, held=None):
    rows, width = queries.shape
    more = [after] + (list(held) if held else [])
    return pl.pallas_call(
        functools.partial(local_kernel, held is None),
        in_specs=[VMEM] * 3 + [HBM] + [VMEM] * (len(more) - 1),
        out_specs=[VMEM] * 3,
        out_shape=[
            jax.ShapeDtypeStruct((rows, width), jnp.float32),
            jax.ShapeDtypeStruct((width // HD, HD, HD), jnp.float32),
            jax.ShapeDtypeStruct((BLOCK, width), queries.dtype),
        ],
        input_output_aliases={4 + i: i for i in range(3)} if held else {},
        compiler_params=grant(LOCAL_MIB),
        cost_estimate=pl.CostEstimate(flops=4 * rows * BLOCK * width, bytes_accessed=10 * rows * width, transcendentals=0),
        name="local",
    )(queries, keys, values, *more)


def mixed_kernel(queries, top_queries, local, prefix, first, mixed, squares, held, sem):
    tiles = BLOCK // HD
    rest = pltpu.make_async_copy(queries.at[pl.ds(BLOCK, BLOCK)], held, sem)
    rest.start()
    for i in range(local.shape[0] // BLOCK):
        if i:
            rest.wait()
        rows = slice(i * BLOCK, (i + 1) * BLOCK)
        acc = None
        for h in range(local.shape[1] // HD):
            cols = head_columns(h)
            state = prefix[h] + first[h] if i else prefix[h]
            q = held[:, cols] if i else top_queries[:, cols]
            m = jnp.dot(q, state.astype(jnp.bfloat16), preferred_element_type=jnp.float32) + local[rows, cols]
            mixed[rows, cols] = m
            acc = m * m if h == 0 else acc + m * m
        turned = jnp.swapaxes(acc.reshape(tiles, HD, HD), 1, 2)
        sums = jnp.sum(turned, axis=1)
        for p in range(PEERS):
            squares[p, i * tiles : (i + 1) * tiles] = sums


def mixed_part(queries, top_queries, local, prefix, first):
    rows, width = queries.shape
    return pl.pallas_call(
        mixed_kernel,
        in_specs=[HBM] + [VMEM] * 4,
        out_specs=[VMEM] * 2,
        out_shape=[
            jax.ShapeDtypeStruct((rows, width), jnp.float32),
            jax.ShapeDtypeStruct((PEERS, rows // HD, HD), jnp.float32),
        ],
        scratch_shapes=[pltpu.VMEM((BLOCK, width), queries.dtype), pltpu.SemaphoreType.DMA(())],
        compiler_params=grant(MIXED_MIB),
        cost_estimate=pl.CostEstimate(flops=2 * rows * HD * width, bytes_accessed=10 * rows * width, transcendentals=0),
        name="mixed",
    )(queries, top_queries, local, prefix, first)


def scored_kernel(mixed, squares, gain, out, rows, sems):
    total = squares[0]
    for p in range(1, PEERS):
        total = total + squares[p]
    scale = lax.rsqrt(total / D + 1e-06)
    copies = []
    for t in range(mixed.shape[0] // HD):
        at = slice(t * HD, (t + 1) * HD)
        column = jnp.swapaxes(jnp.broadcast_to(scale[t : t + 1], (HD, HD)), 0, 1)
        for h in range(mixed.shape[1] // HD):
            cols = head_columns(h)
            rows[at, cols] = (mixed[at, cols] * column * gain[:, cols]).astype(jnp.bfloat16)
        part = pl.ds(t * HD, HD)
        copies.append(pltpu.make_async_copy(rows.at[part], out.at[part], sems.at[t]))
        copies[-1].start()
    for copy in copies:
        copy.wait()


def scored_part(mixed, squares, gain):
    rows, width = mixed.shape
    return pl.pallas_call(
        scored_kernel,
        in_specs=[VMEM] * 3,
        out_specs=HBM,
        out_shape=jax.ShapeDtypeStruct((rows, width), jnp.bfloat16),
        scratch_shapes=[pltpu.VMEM((rows, width), jnp.bfloat16), pltpu.SemaphoreType.DMA((rows // HD,))],
        compiler_params=grant(OTHER_MIB),
        name="scored",
    )(mixed, squares, gain.reshape(1, width))


def shards(queries, keys, values, gain):
    total = shard_state(keys, values)
    prefix, (local, first, top_queries) = exclusive_states(total, functools.partial(local_part, queries, keys, values))
    mixed, squares = mixed_part(queries, top_queries, local, prefix, first)
    squares = lax.all_to_all(squares, "tp", 0, 0)
    return scored_part(mixed, squares, gain)


def solution(mesh):
    return jax.shard_map(
        shards,
        mesh=mesh,
        in_specs=(P("ctx", "tp"), P("ctx", "tp"), P("ctx", "tp"), P("tp")),
        out_specs=P("ctx", "tp"),
        check_vma=False,
    )
```

```python
import functools

import jax
import jax.numpy as jnp
from jax import lax
from jax.experimental import pallas as pl
from jax.experimental.pallas import tpu as pltpu
from jax.sharding import PartitionSpec as P

HD = 128
D = 4096
BLOCK = 512
XS = 4
ZS = 16
NEAR = 4
FAR = ZS // NEAR
MEMBERS = XS * NEAR
PEERS = 8
LOAD = 512
CHUNK = 512
STORE = 128
VMEM = pl.BlockSpec(memory_space=pltpu.VMEM)
HBM = pl.BlockSpec(memory_space=pltpu.HBM)
STATE_MIB = 53.2
LOCAL_MIB = 32
EARLY = 1
MIXED_MIB = 32
OTHER_MIB = 32


def grant(mib):
    return pltpu.CompilerParams(vmem_limit_bytes=int(mib * 1024 * 1024))


def near_groups():
    return [[x * ZS + a * NEAR + b for x in range(XS) for b in range(NEAR)] for a in range(FAR)]


def between(pairs):
    return [(x * ZS + i * NEAR + b, x * ZS + j * NEAR + b) for x in range(XS) for b in range(NEAR) for i, j in pairs]


def contract_tokens(left, right):
    return lax.dot_general(left, right, (((0,), (0,)), ((), ())), preferred_element_type=jnp.float32)


def contract_last(left, right):
    return lax.dot_general(left, right, (((1,), (1,)), ((), ())), preferred_element_type=jnp.float32)


def head_columns(h):
    return slice(h * HD, (h + 1) * HD)


def state_kernel(keys, values, total, key_rows, value_rows, sems):
    rows, width = keys.shape
    parts = rows // LOAD
    copies = []
    for c in range(parts):
        at = pl.ds(c * LOAD, LOAD)
        pair = (
            pltpu.make_async_copy(keys.at[at], key_rows.at[at], sems.at[c]),
            pltpu.make_async_copy(values.at[at], value_rows.at[at], sems.at[parts + c]),
        )
        for copy in pair:
            copy.start()
        copies.append(pair)
    sums = [None] * (width // HD)
    for c in range(0, rows, CHUNK):
        for pair in copies[c // LOAD : (c + CHUNK) // LOAD]:
            for copy in pair:
                copy.wait()
        for h in range(len(sums)):
            cols = head_columns(h)
            part = contract_tokens(key_rows[c : c + CHUNK, cols], value_rows[c : c + CHUNK, cols])
            sums[h] = part if c == 0 else sums[h] + part
    for h, s in enumerate(sums):
        total[h] = s


def shard_state(keys, values):
    rows, width = keys.shape
    return pl.pallas_call(
        state_kernel,
        in_specs=[HBM, HBM],
        out_specs=VMEM,
        out_shape=jax.ShapeDtypeStruct((width // HD, HD, HD), jnp.float32),
        scratch_shapes=[
            pltpu.VMEM((rows, width), keys.dtype),
            pltpu.VMEM((rows, width), values.dtype),
            pltpu.SemaphoreType.DMA((2 * rows // LOAD,)),
        ],
        compiler_params=grant(STATE_MIB),
        cost_estimate=pl.CostEstimate(flops=2 * rows * width * HD, bytes_accessed=4 * rows * width, transcendentals=0),
        name="states",
    )(keys, values)


STEPS = (
    ((2, 0),),
    ((2, 1), (3, 0),),
    ((0, 3), (1, 0),),
    ((0, 1), (2, 3),),
    ((1, 3), (3, 1),),
    ((1, 2),),
    ((3, 2),),
)
RELAY = len(STEPS) - 1
CARRIED = 2
WITH = (1, 0)
LOCAL_AFTER = 0


def relay_kernel(own, *rest):
    carried, out = rest[len(WITH)], rest[-1]
    src, dst = STEPS[RELAY][0]
    for x in range(XS):
        if src < dst:
            out[x] = own[x] + carried[x]
        else:
            out[x] = own[x - 1] + carried[x] if x else carried[x]


def rows_sent(step):
    return XS if any(src < dst for src, dst in STEPS[step]) or step == RELAY else XS - 1


def own_kernel(got, *outs):
    run = None
    for x in range(XS):
        for b in range(NEAR):
            run = got[x * NEAR + b] if run is None else run + got[x * NEAR + b]
        for out in outs:
            if x < out.shape[0]:
                out[x] = run


def back_kernel(meanwhile, got, *rest):
    parts, back = rest[:-1], rest[-1]
    mine = (lax.axis_index("ctx") // NEAR) % FAR
    run = None
    for x in range(XS):
        start = jnp.zeros(got.shape[1:], jnp.float32) if run is None else run
        run = start
        for k, (step, part) in enumerate(zip(STEPS, parts)):
            shifted = [dst for src, dst in step if src > dst and k != RELAY]
            if not shifted:
                start = start + part[x]
            elif len(shifted) == len(step):
                start = start + part[x - 1] if x else start
            else:
                moved = mine == shifted[0]
                for dst in shifted[1:]:
                    moved = moved | (mine == dst)
                before = part[x - 1] if x else jnp.zeros_like(start)
                start = start + jnp.where(moved, before, part[x])
        for b in range(NEAR):
            back[x * NEAR + b] = start
            if b < NEAR - 1:
                start = start + got[x * NEAR + b]
            run = run + got[x * NEAR + b]


def exclusive_states(state, local):
    rows = state.shape[0] * HD // MEMBERS
    pieces = state.reshape(MEMBERS, rows, HD)
    got = lax.all_to_all(pieces, "ctx", 0, 0, axis_index_groups=near_groups())
    sent = pl.pallas_call(
        own_kernel,
        in_specs=[VMEM],
        out_specs=[VMEM] * len(STEPS),
        out_shape=[jax.ShapeDtypeStruct((rows_sent(k), rows, HD), jnp.float32) for k in range(len(STEPS))],
        compiler_params=grant(OTHER_MIB),
        name="sent",
    )(got)
    parts = []
    for k, step in enumerate(STEPS):
        out = sent[k]
        if k == RELAY:
            held = local(sent[0])
            late = [parts[j] for j in (*WITH, CARRIED)] + [held[1]]
            out = pl.pallas_call(
                relay_kernel,
                in_specs=[VMEM] * len(late) + [HBM],
                out_specs=VMEM,
                out_shape=jax.ShapeDtypeStruct(out.shape, jnp.float32),
                compiler_params=grant(OTHER_MIB),
                name="relay",
            )(out, *late)
        parts.append(lax.ppermute(out, "ctx", between(step)))
    held = local(out, held)
    back = pl.pallas_call(
        back_kernel,
        in_specs=[HBM] + [VMEM] * (1 + len(parts)),
        out_specs=VMEM,
        out_shape=jax.ShapeDtypeStruct(got.shape, jnp.float32),
        compiler_params=grant(OTHER_MIB),
        name="back",
    )(held[1], got, *parts)
    mine = lax.all_to_all(back, "ctx", 0, 0, axis_index_groups=near_groups())
    return mine.reshape(state.shape), held


def local_kernel(early, queries, keys, values, *rest):
    out, first, top_queries = rest[-3:]
    leading = (lax.axis_index("ctx") // NEAR) % FAR < EARLY

    @pl.when(leading == early)
    def _():
        local_work(queries, keys, values, out, first, top_queries)


def local_work(queries, keys, values, out, first, top_queries):
    half = BLOCK // 2
    row = lax.broadcasted_iota(jnp.int32, (half, half), 0)
    col = lax.broadcasted_iota(jnp.int32, (half, half), 1)
    lower = row >= col
    top_queries[...] = queries[:BLOCK]
    for h in range(queries.shape[1] // HD):
        cols = head_columns(h)
        first[h] = contract_tokens(keys[:BLOCK, cols], values[:BLOCK, cols])
        for start in range(0, queries.shape[0], BLOCK):
            top_rows = slice(start, start + half)
            low_rows = slice(start + half, start + BLOCK)
            q, k = queries[top_rows, cols], keys[top_rows, cols]
            top = jnp.where(lower, contract_last(q, k), 0.0).astype(jnp.bfloat16)
            out[top_rows, cols] = jnp.dot(top, values[top_rows, cols], preferred_element_type=jnp.float32)
            q = queries[low_rows, cols]
            side = contract_last(q, k).astype(jnp.bfloat16)
            low = jnp.where(lower, contract_last(q, keys[low_rows, cols]), 0.0).astype(jnp.bfloat16)
            both = jnp.concatenate([side, low], axis=1)
            v = values[start : start + BLOCK, cols]
            out[low_rows, cols] = jnp.dot(both, v, preferred_element_type=jnp.float32)


def local_part(queries, keys, values, after, held=None):
    rows, width = queries.shape
    more = [after] + (list(held) if held else [])
    return pl.pallas_call(
        functools.partial(local_kernel, held is None),
        in_specs=[VMEM] * 3 + [HBM] + [VMEM] * (len(more) - 1),
        out_specs=[VMEM] * 3,
        out_shape=[
            jax.ShapeDtypeStruct((rows, width), jnp.float32),
            jax.ShapeDtypeStruct((width // HD, HD, HD), jnp.float32),
            jax.ShapeDtypeStruct((BLOCK, width), queries.dtype),
        ],
        input_output_aliases={4 + i: i for i in range(3)} if held else {},
        compiler_params=grant(LOCAL_MIB),
        cost_estimate=pl.CostEstimate(flops=4 * rows * BLOCK * width, bytes_accessed=10 * rows * width, transcendentals=0),
        name="local",
    )(queries, keys, values, *more)


def mixed_kernel(queries, top_queries, local, prefix, first, mixed, squares, held, sem):
    tiles = BLOCK // HD
    rest = pltpu.make_async_copy(queries.at[pl.ds(BLOCK, BLOCK)], held, sem)
    rest.start()
    for i in range(local.shape[0] // BLOCK):
        if i:
            rest.wait()
        rows = slice(i * BLOCK, (i + 1) * BLOCK)
        acc = None
        for h in range(local.shape[1] // HD):
            cols = head_columns(h)
            state = prefix[h] + first[h] if i else prefix[h]
            q = held[:, cols] if i else top_queries[:, cols]
            m = jnp.dot(q, state.astype(jnp.bfloat16), preferred_element_type=jnp.float32) + local[rows, cols]
            mixed[rows, cols] = m
            acc = m * m if h == 0 else acc + m * m
        turned = jnp.swapaxes(acc.reshape(tiles, HD, HD), 1, 2)
        sums = jnp.sum(turned, axis=1)
        for p in range(PEERS):
            squares[p, i * tiles : (i + 1) * tiles] = sums


def mixed_part(queries, top_queries, local, prefix, first):
    rows, width = queries.shape
    return pl.pallas_call(
        mixed_kernel,
        in_specs=[HBM] + [VMEM] * 4,
        out_specs=[VMEM] * 2,
        out_shape=[
            jax.ShapeDtypeStruct((rows, width), jnp.float32),
            jax.ShapeDtypeStruct((PEERS, rows // HD, HD), jnp.float32),
        ],
        scratch_shapes=[pltpu.VMEM((BLOCK, width), queries.dtype), pltpu.SemaphoreType.DMA(())],
        compiler_params=grant(MIXED_MIB),
        cost_estimate=pl.CostEstimate(flops=2 * rows * HD * width, bytes_accessed=10 * rows * width, transcendentals=0),
        name="mixed",
    )(queries, top_queries, local, prefix, first)


def scored_kernel(mixed, squares, gain, out, rows, sems):
    total = squares[0]
    for p in range(1, PEERS):
        total = total + squares[p]
    scale = lax.rsqrt(total / D + 1e-06)
    copies = []
    for t in range(mixed.shape[0] // HD):
        at = slice(t * HD, (t + 1) * HD)
        column = jnp.swapaxes(jnp.broadcast_to(scale[t : t + 1], (HD, HD)), 0, 1)
        for h in range(mixed.shape[1] // HD):
            cols = head_columns(h)
            rows[at, cols] = (mixed[at, cols] * column * gain[:, cols]).astype(jnp.bfloat16)
        part = pl.ds(t * HD, HD)
        copies.append(pltpu.make_async_copy(rows.at[part], out.at[part], sems.at[t]))
        copies[-1].start()
    for copy in copies:
        copy.wait()


def scored_part(mixed, squares, gain):
    rows, width = mixed.shape
    return pl.pallas_call(
        scored_kernel,
        in_specs=[VMEM] * 3,
        out_specs=HBM,
        out_shape=jax.ShapeDtypeStruct((rows, width), jnp.bfloat16),
        scratch_shapes=[pltpu.VMEM((rows, width), jnp.bfloat16), pltpu.SemaphoreType.DMA((rows // HD,))],
        compiler_params=grant(OTHER_MIB),
        name="scored",
    )(mixed, squares, gain.reshape(1, width))


def shards(queries, keys, values, gain):
    total = shard_state(keys, values)
    prefix, (local, first, top_queries) = exclusive_states(total, functools.partial(local_part, queries, keys, values))
    mixed, squares = mixed_part(queries, top_queries, local, prefix, first)
    squares = lax.all_to_all(squares, "tp", 0, 0)
    return scored_part(mixed, squares, gain)


def solution(mesh):
    return jax.shard_map(
        shards,
        mesh=mesh,
        in_specs=(P("ctx", "tp"), P("ctx", "tp"), P("ctx", "tp"), P("tp")),
        out_specs=P("ctx", "tp"),
        check_vma=False,
    )
```

```python
import functools

import jax
import jax.numpy as jnp
from jax import lax
from jax.experimental import pallas as pl
from jax.experimental.pallas import tpu as pltpu
from jax.sharding import PartitionSpec as P

HD = 128
D = 4096
BLOCK = 512
XS = 4
ZS = 16
NEAR = 4
FAR = ZS // NEAR
MEMBERS = XS * NEAR
PEERS = 8
LOAD = 512
CHUNK = 512
STORE = 128
VMEM = pl.BlockSpec(memory_space=pltpu.VMEM)
HBM = pl.BlockSpec(memory_space=pltpu.HBM)
STATE_MIB = 53.2
LOCAL_MIB = 32
EARLY = 1
MIXED_MIB = 32
OTHER_MIB = 32


def grant(mib):
    return pltpu.CompilerParams(vmem_limit_bytes=int(mib * 1024 * 1024))


def near_groups():
    return [[x * ZS + a * NEAR + b for x in range(XS) for b in range(NEAR)] for a in range(FAR)]


def between(pairs):
    return [(x * ZS + i * NEAR + b, x * ZS + j * NEAR + b) for x in range(XS) for b in range(NEAR) for i, j in pairs]


def contract_tokens(left, right):
    return lax.dot_general(left, right, (((0,), (0,)), ((), ())), preferred_element_type=jnp.float32)


def contract_last(left, right):
    return lax.dot_general(left, right, (((1,), (1,)), ((), ())), preferred_element_type=jnp.float32)


def head_columns(h):
    return slice(h * HD, (h + 1) * HD)


def state_kernel(keys, values, total, key_rows, value_rows, sems):
    rows, width = keys.shape
    parts = rows // LOAD
    copies = []
    for c in range(parts):
        at = pl.ds(c * LOAD, LOAD)
        pair = (
            pltpu.make_async_copy(keys.at[at], key_rows.at[at], sems.at[c]),
            pltpu.make_async_copy(values.at[at], value_rows.at[at], sems.at[parts + c]),
        )
        for copy in pair:
            copy.start()
        copies.append(pair)
    sums = [None] * (width // HD)
    for c in range(0, rows, CHUNK):
        for pair in copies[c // LOAD : (c + CHUNK) // LOAD]:
            for copy in pair:
                copy.wait()
        for h in range(len(sums)):
            cols = head_columns(h)
            part = contract_tokens(key_rows[c : c + CHUNK, cols], value_rows[c : c + CHUNK, cols])
            sums[h] = part if c == 0 else sums[h] + part
    for h, s in enumerate(sums):
        total[h] = s


def shard_state(keys, values):
    rows, width = keys.shape
    return pl.pallas_call(
        state_kernel,
        in_specs=[HBM, HBM],
        out_specs=VMEM,
        out_shape=jax.ShapeDtypeStruct((width // HD, HD, HD), jnp.float32),
        scratch_shapes=[
            pltpu.VMEM((rows, width), keys.dtype),
            pltpu.VMEM((rows, width), values.dtype),
            pltpu.SemaphoreType.DMA((2 * rows // LOAD,)),
        ],
        compiler_params=grant(STATE_MIB),
        cost_estimate=pl.CostEstimate(flops=2 * rows * width * HD, bytes_accessed=4 * rows * width, transcendentals=0),
        name="states",
    )(keys, values)


STEPS = (
    ((2, 0),),
    ((3, 0),),
    ((0, 3), (1, 0), (2, 1),),
    ((0, 1), (2, 3),),
    ((1, 3), (3, 1),),
    ((1, 2),),
    ((3, 2),),
)
RELAY = len(STEPS) - 1
CARRIED = 2
WITH = (1, 0)
LOCAL_AFTER = 0


def relay_kernel(own, *rest):
    carried, out = rest[len(WITH)], rest[-1]
    src, dst = STEPS[RELAY][0]
    for x in range(XS):
        if src < dst:
            out[x] = own[x] + carried[x]
        else:
            out[x] = own[x - 1] + carried[x] if x else carried[x]


def rows_sent(step):
    return XS if any(src < dst for src, dst in STEPS[step]) or step == RELAY else XS - 1


def own_kernel(got, *outs):
    run = None
    for x in range(XS):
        for b in range(NEAR):
            run = got[x * NEAR + b] if run is None else run + got[x * NEAR + b]
        for out in outs:
            if x < out.shape[0]:
                out[x] = run


def back_kernel(meanwhile, got, *rest):
    parts, back = rest[:-1], rest[-1]
    mine = (lax.axis_index("ctx") // NEAR) % FAR
    run = None
    for x in range(XS):
        start = jnp.zeros(got.shape[1:], jnp.float32) if run is None else run
        run = start
        for k, (step, part) in enumerate(zip(STEPS, parts)):
            shifted = [dst for src, dst in step if src > dst and k != RELAY]
            if not shifted:
                start = start + part[x]
            elif len(shifted) == len(step):
                start = start + part[x - 1] if x else start
            else:
                moved = mine == shifted[0]
                for dst in shifted[1:]:
                    moved = moved | (mine == dst)
                before = part[x - 1] if x else jnp.zeros_like(start)
                start = start + jnp.where(moved, before, part[x])
        for b in range(NEAR):
            back[x * NEAR + b] = start
            if b < NEAR - 1:
                start = start + got[x * NEAR + b]
            run = run + got[x * NEAR + b]


def exclusive_states(state, local):
    rows = state.shape[0] * HD // MEMBERS
    pieces = state.reshape(MEMBERS, rows, HD)
    got = lax.all_to_all(pieces, "ctx", 0, 0, axis_index_groups=near_groups())
    sent = pl.pallas_call(
        own_kernel,
        in_specs=[VMEM],
        out_specs=[VMEM] * len(STEPS),
        out_shape=[jax.ShapeDtypeStruct((rows_sent(k), rows, HD), jnp.float32) for k in range(len(STEPS))],
        compiler_params=grant(OTHER_MIB),
        name="sent",
    )(got)
    parts = []
    for k, step in enumerate(STEPS):
        out = sent[k]
        if k == RELAY:
            held = local(sent[0])
            late = [parts[j] for j in (*WITH, CARRIED)] + [held[1]]
            out = pl.pallas_call(
                relay_kernel,
                in_specs=[VMEM] * len(late) + [HBM],
                out_specs=VMEM,
                out_shape=jax.ShapeDtypeStruct(out.shape, jnp.float32),
                compiler_params=grant(OTHER_MIB),
                name="relay",
            )(out, *late)
        parts.append(lax.ppermute(out, "ctx", between(step)))
    held = local(out, held)
    back = pl.pallas_call(
        back_kernel,
        in_specs=[HBM] + [VMEM] * (1 + len(parts)),
        out_specs=VMEM,
        out_shape=jax.ShapeDtypeStruct(got.shape, jnp.float32),
        compiler_params=grant(OTHER_MIB),
        name="back",
    )(held[1], got, *parts)
    mine = lax.all_to_all(back, "ctx", 0, 0, axis_index_groups=near_groups())
    return mine.reshape(state.shape), held


def local_kernel(early, queries, keys, values, *rest):
    out, first, top_queries = rest[-3:]
    leading = (lax.axis_index("ctx") // NEAR) % FAR < EARLY

    @pl.when(leading == early)
    def _():
        local_work(queries, keys, values, out, first, top_queries)


def local_work(queries, keys, values, out, first, top_queries):
    half = BLOCK // 2
    row = lax.broadcasted_iota(jnp.int32, (half, half), 0)
    col = lax.broadcasted_iota(jnp.int32, (half, half), 1)
    lower = row >= col
    top_queries[...] = queries[:BLOCK]
    for h in range(queries.shape[1] // HD):
        cols = head_columns(h)
        first[h] = contract_tokens(keys[:BLOCK, cols], values[:BLOCK, cols])
        for start in range(0, queries.shape[0], BLOCK):
            top_rows = slice(start, start + half)
            low_rows = slice(start + half, start + BLOCK)
            q, k = queries[top_rows, cols], keys[top_rows, cols]
            top = jnp.where(lower, contract_last(q, k), 0.0).astype(jnp.bfloat16)
            out[top_rows, cols] = jnp.dot(top, values[top_rows, cols], preferred_element_type=jnp.float32)
            q = queries[low_rows, cols]
            side = contract_last(q, k).astype(jnp.bfloat16)
            low = jnp.where(lower, contract_last(q, keys[low_rows, cols]), 0.0).astype(jnp.bfloat16)
            both = jnp.concatenate([side, low], axis=1)
            v = values[start : start + BLOCK, cols]
            out[low_rows, cols] = jnp.dot(both, v, preferred_element_type=jnp.float32)


def local_part(queries, keys, values, after, held=None):
    rows, width = queries.shape
    more = [after] + (list(held) if held else [])
    return pl.pallas_call(
        functools.partial(local_kernel, held is None),
        in_specs=[VMEM] * 3 + [HBM] + [VMEM] * (len(more) - 1),
        out_specs=[VMEM] * 3,
        out_shape=[
            jax.ShapeDtypeStruct((rows, width), jnp.float32),
            jax.ShapeDtypeStruct((width // HD, HD, HD), jnp.float32),
            jax.ShapeDtypeStruct((BLOCK, width), queries.dtype),
        ],
        input_output_aliases={4 + i: i for i in range(3)} if held else {},
        compiler_params=grant(LOCAL_MIB),
        cost_estimate=pl.CostEstimate(flops=4 * rows * BLOCK * width, bytes_accessed=10 * rows * width, transcendentals=0),
        name="local",
    )(queries, keys, values, *more)


def mixed_kernel(queries, top_queries, local, prefix, first, mixed, squares, held, sem):
    tiles = BLOCK // HD
    rest = pltpu.make_async_copy(queries.at[pl.ds(BLOCK, BLOCK)], held, sem)
    rest.start()
    for i in range(local.shape[0] // BLOCK):
        if i:
            rest.wait()
        rows = slice(i * BLOCK, (i + 1) * BLOCK)
        acc = None
        for h in range(local.shape[1] // HD):
            cols = head_columns(h)
            state = prefix[h] + first[h] if i else prefix[h]
            q = held[:, cols] if i else top_queries[:, cols]
            m = jnp.dot(q, state.astype(jnp.bfloat16), preferred_element_type=jnp.float32) + local[rows, cols]
            mixed[rows, cols] = m
            acc = m * m if h == 0 else acc + m * m
        turned = jnp.swapaxes(acc.reshape(tiles, HD, HD), 1, 2)
        sums = jnp.sum(turned, axis=1)
        for p in range(PEERS):
            squares[p, i * tiles : (i + 1) * tiles] = sums


def mixed_part(queries, top_queries, local, prefix, first):
    rows, width = queries.shape
    return pl.pallas_call(
        mixed_kernel,
        in_specs=[HBM] + [VMEM] * 4,
        out_specs=[VMEM] * 2,
        out_shape=[
            jax.ShapeDtypeStruct((rows, width), jnp.float32),
            jax.ShapeDtypeStruct((PEERS, rows // HD, HD), jnp.float32),
        ],
        scratch_shapes=[pltpu.VMEM((BLOCK, width), queries.dtype), pltpu.SemaphoreType.DMA(())],
        compiler_params=grant(MIXED_MIB),
        cost_estimate=pl.CostEstimate(flops=2 * rows * HD * width, bytes_accessed=10 * rows * width, transcendentals=0),
        name="mixed",
    )(queries, top_queries, local, prefix, first)


def scored_kernel(mixed, squares, gain, out, rows, sems):
    total = squares[0]
    for p in range(1, PEERS):
        total = total + squares[p]
    scale = lax.rsqrt(total / D + 1e-06)
    copies = []
    for t in range(mixed.shape[0] // HD):
        at = slice(t * HD, (t + 1) * HD)
        column = jnp.swapaxes(jnp.broadcast_to(scale[t : t + 1], (HD, HD)), 0, 1)
        for h in range(mixed.shape[1] // HD):
            cols = head_columns(h)
            rows[at, cols] = (mixed[at, cols] * column * gain[:, cols]).astype(jnp.bfloat16)
        part = pl.ds(t * HD, HD)
        copies.append(pltpu.make_async_copy(rows.at[part], out.at[part], sems.at[t]))
        copies[-1].start()
    for copy in copies:
        copy.wait()


def scored_part(mixed, squares, gain):
    rows, width = mixed.shape
    return pl.pallas_call(
        scored_kernel,
        in_specs=[VMEM] * 3,
        out_specs=HBM,
        out_shape=jax.ShapeDtypeStruct((rows, width), jnp.bfloat16),
        scratch_shapes=[pltpu.VMEM((rows, width), jnp.bfloat16), pltpu.SemaphoreType.DMA((rows // HD,))],
        compiler_params=grant(OTHER_MIB),
        name="scored",
    )(mixed, squares, gain.reshape(1, width))


def shards(queries, keys, values, gain):
    total = shard_state(keys, values)
    prefix, (local, first, top_queries) = exclusive_states(total, functools.partial(local_part, queries, keys, values))
    mixed, squares = mixed_part(queries, top_queries, local, prefix, first)
    squares = lax.all_to_all(squares, "tp", 0, 0)
    return scored_part(mixed, squares, gain)


def solution(mesh):
    return jax.shard_map(
        shards,
        mesh=mesh,
        in_specs=(P("ctx", "tp"), P("ctx", "tp"), P("ctx", "tp"), P("tp")),
        out_specs=P("ctx", "tp"),
        check_vma=False,
    )
```

```python
import functools

import jax
import jax.numpy as jnp
from jax import lax
from jax.experimental import pallas as pl
from jax.experimental.pallas import tpu as pltpu
from jax.sharding import PartitionSpec as P

HD = 128
D = 4096
BLOCK = 512
KEPT = 640
XS = 4
ZS = 16
NEAR = 4
FAR = ZS // NEAR
MEMBERS = XS * NEAR
PEERS = 8
LOAD = 512
CHUNK = 512
STORE = 128
VMEM = pl.BlockSpec(memory_space=pltpu.VMEM)
HBM = pl.BlockSpec(memory_space=pltpu.HBM)
STATE_MIB = 53.2
LOCAL_MIB = 32
EARLY = 1
MIXED_MIB = 32
OTHER_MIB = 32


def grant(mib):
    return pltpu.CompilerParams(vmem_limit_bytes=int(mib * 1024 * 1024))


def near_groups():
    return [[x * ZS + a * NEAR + b for x in range(XS) for b in range(NEAR)] for a in range(FAR)]


def between(pairs):
    return [(x * ZS + i * NEAR + b, x * ZS + j * NEAR + b) for x in range(XS) for b in range(NEAR) for i, j in pairs]


def contract_tokens(left, right):
    return lax.dot_general(left, right, (((0,), (0,)), ((), ())), preferred_element_type=jnp.float32)


def contract_last(left, right):
    return lax.dot_general(left, right, (((1,), (1,)), ((), ())), preferred_element_type=jnp.float32)


def head_columns(h):
    return slice(h * HD, (h + 1) * HD)


def state_kernel(keys, values, total, key_rows, value_rows, sems):
    rows, width = keys.shape
    parts = rows // LOAD
    copies = []
    for c in range(parts):
        at = pl.ds(c * LOAD, LOAD)
        pair = (
            pltpu.make_async_copy(keys.at[at], key_rows.at[at], sems.at[c]),
            pltpu.make_async_copy(values.at[at], value_rows.at[at], sems.at[parts + c]),
        )
        for copy in pair:
            copy.start()
        copies.append(pair)
    sums = [None] * (width // HD)
    for c in range(0, rows, CHUNK):
        for pair in copies[c // LOAD : (c + CHUNK) // LOAD]:
            for copy in pair:
                copy.wait()
        for h in range(len(sums)):
            cols = head_columns(h)
            part = contract_tokens(key_rows[c : c + CHUNK, cols], value_rows[c : c + CHUNK, cols])
            sums[h] = part if c == 0 else sums[h] + part
    for h, s in enumerate(sums):
        total[h] = s


def shard_state(keys, values):
    rows, width = keys.shape
    return pl.pallas_call(
        state_kernel,
        in_specs=[HBM, HBM],
        out_specs=VMEM,
        out_shape=jax.ShapeDtypeStruct((width // HD, HD, HD), jnp.float32),
        scratch_shapes=[
            pltpu.VMEM((rows, width), keys.dtype),
            pltpu.VMEM((rows, width), values.dtype),
            pltpu.SemaphoreType.DMA((2 * rows // LOAD,)),
        ],
        compiler_params=grant(STATE_MIB),
        cost_estimate=pl.CostEstimate(flops=2 * rows * width * HD, bytes_accessed=4 * rows * width, transcendentals=0),
        name="states",
    )(keys, values)


STEPS = (
    ((2, 0),),
    ((2, 1), (3, 0),),
    ((0, 3), (1, 0),),
    ((0, 1), (2, 3),),
    ((1, 3), (3, 1),),
    ((1, 2),),
    ((3, 2),),
)
RELAY = len(STEPS) - 1
CARRIED = 2
WITH = (1, 0)
LOCAL_AFTER = 0


def relay_kernel(own, *rest):
    carried, out = rest[len(WITH)], rest[-1]
    src, dst = STEPS[RELAY][0]
    for x in range(XS):
        if src < dst:
            out[x] = own[x] + carried[x]
        else:
            out[x] = own[x - 1] + carried[x] if x else carried[x]


def rows_sent(step):
    return XS if any(src < dst for src, dst in STEPS[step]) or step == RELAY else XS - 1


def own_kernel(got, *outs):
    run = None
    for x in range(XS):
        for b in range(NEAR):
            run = got[x * NEAR + b] if run is None else run + got[x * NEAR + b]
        for out in outs:
            if x < out.shape[0]:
                out[x] = run


def back_kernel(meanwhile, got, *rest):
    parts, back = rest[:-1], rest[-1]
    mine = (lax.axis_index("ctx") // NEAR) % FAR
    run = None
    for x in range(XS):
        start = jnp.zeros(got.shape[1:], jnp.float32) if run is None else run
        run = start
        for k, (step, part) in enumerate(zip(STEPS, parts)):
            shifted = [dst for src, dst in step if src > dst and k != RELAY]
            if not shifted:
                start = start + part[x]
            elif len(shifted) == len(step):
                start = start + part[x - 1] if x else start
            else:
                moved = mine == shifted[0]
                for dst in shifted[1:]:
                    moved = moved | (mine == dst)
                before = part[x - 1] if x else jnp.zeros_like(start)
                start = start + jnp.where(moved, before, part[x])
        for b in range(NEAR):
            back[x * NEAR + b] = start
            if b < NEAR - 1:
                start = start + got[x * NEAR + b]
            run = run + got[x * NEAR + b]


def exclusive_states(state, local):
    rows = state.shape[0] * HD // MEMBERS
    pieces = state.reshape(MEMBERS, rows, HD)
    got = lax.all_to_all(pieces, "ctx", 0, 0, axis_index_groups=near_groups())
    sent = pl.pallas_call(
        own_kernel,
        in_specs=[VMEM],
        out_specs=[VMEM] * len(STEPS),
        out_shape=[jax.ShapeDtypeStruct((rows_sent(k), rows, HD), jnp.float32) for k in range(len(STEPS))],
        compiler_params=grant(OTHER_MIB),
        name="sent",
    )(got)
    parts = []
    for k, step in enumerate(STEPS):
        out = sent[k]
        if k == RELAY:
            held = local(sent[0])
            late = [parts[j] for j in (*WITH, CARRIED)] + [held[1]]
            out = pl.pallas_call(
                relay_kernel,
                in_specs=[VMEM] * len(late) + [HBM],
                out_specs=VMEM,
                out_shape=jax.ShapeDtypeStruct(out.shape, jnp.float32),
                compiler_params=grant(OTHER_MIB),
                name="relay",
            )(out, *late)
        parts.append(lax.ppermute(out, "ctx", between(step)))
    held = local(out, held)
    back = pl.pallas_call(
        back_kernel,
        in_specs=[HBM] + [VMEM] * (1 + len(parts)),
        out_specs=VMEM,
        out_shape=jax.ShapeDtypeStruct(got.shape, jnp.float32),
        compiler_params=grant(OTHER_MIB),
        name="back",
    )(held[1], got, *parts)
    mine = lax.all_to_all(back, "ctx", 0, 0, axis_index_groups=near_groups())
    return mine.reshape(state.shape), held


def local_kernel(early, queries, keys, values, *rest):
    out, first, top_queries = rest[-3:]
    leading = (lax.axis_index("ctx") // NEAR) % FAR < EARLY

    @pl.when(leading == early)
    def _():
        local_work(queries, keys, values, out, first, top_queries)


def local_work(queries, keys, values, out, first, top_queries):
    half = BLOCK // 2
    row = lax.broadcasted_iota(jnp.int32, (half, half), 0)
    col = lax.broadcasted_iota(jnp.int32, (half, half), 1)
    lower = row >= col
    top_queries[...] = queries[:KEPT]
    for h in range(queries.shape[1] // HD):
        cols = head_columns(h)
        first[h] = contract_tokens(keys[:BLOCK, cols], values[:BLOCK, cols])
        for start in range(0, queries.shape[0], BLOCK):
            top_rows = slice(start, start + half)
            low_rows = slice(start + half, start + BLOCK)
            q, k = queries[top_rows, cols], keys[top_rows, cols]
            top = jnp.where(lower, contract_last(q, k), 0.0).astype(jnp.bfloat16)
            out[top_rows, cols] = jnp.dot(top, values[top_rows, cols], preferred_element_type=jnp.float32)
            q = queries[low_rows, cols]
            side = contract_last(q, k).astype(jnp.bfloat16)
            low = jnp.where(lower, contract_last(q, keys[low_rows, cols]), 0.0).astype(jnp.bfloat16)
            both = jnp.concatenate([side, low], axis=1)
            v = values[start : start + BLOCK, cols]
            out[low_rows, cols] = jnp.dot(both, v, preferred_element_type=jnp.float32)


def local_part(queries, keys, values, after, held=None):
    rows, width = queries.shape
    more = [after] + (list(held) if held else [])
    return pl.pallas_call(
        functools.partial(local_kernel, held is None),
        in_specs=[VMEM] * 3 + [HBM] + [VMEM] * (len(more) - 1),
        out_specs=[VMEM] * 3,
        out_shape=[
            jax.ShapeDtypeStruct((rows, width), jnp.float32),
            jax.ShapeDtypeStruct((width // HD, HD, HD), jnp.float32),
            jax.ShapeDtypeStruct((KEPT, width), queries.dtype),
        ],
        input_output_aliases={4 + i: i for i in range(3)} if held else {},
        compiler_params=grant(LOCAL_MIB),
        cost_estimate=pl.CostEstimate(flops=4 * rows * BLOCK * width, bytes_accessed=10 * rows * width, transcendentals=0),
        name="local",
    )(queries, keys, values, *more)


def mixed_kernel(queries, top_queries, local, prefix, first, mixed, squares, held, sem):
    rows = local.shape[0]
    rest = pltpu.make_async_copy(queries.at[pl.ds(KEPT, rows - KEPT)], held, sem)
    rest.start()
    for low_row, high_row in ((0, BLOCK), (BLOCK, KEPT), (KEPT, rows)):
        if low_row == KEPT:
            rest.wait()
        part = slice(low_row, high_row)
        tiles = (high_row - low_row) // HD
        acc = None
        for h in range(local.shape[1] // HD):
            cols = head_columns(h)
            state = prefix[h] + first[h] if low_row else prefix[h]
            q = held[:, cols] if low_row == KEPT else top_queries[part, cols]
            m = jnp.dot(q, state.astype(jnp.bfloat16), preferred_element_type=jnp.float32) + local[part, cols]
            mixed[part, cols] = m
            acc = m * m if h == 0 else acc + m * m
        turned = jnp.swapaxes(acc.reshape(tiles, HD, HD), 1, 2)
        sums = jnp.sum(turned, axis=1)
        for p in range(PEERS):
            squares[p, low_row // HD : high_row // HD] = sums


def mixed_part(queries, top_queries, local, prefix, first):
    rows, width = queries.shape
    return pl.pallas_call(
        mixed_kernel,
        in_specs=[HBM] + [VMEM] * 4,
        out_specs=[VMEM] * 2,
        out_shape=[
            jax.ShapeDtypeStruct((rows, width), jnp.float32),
            jax.ShapeDtypeStruct((PEERS, rows // HD, HD), jnp.float32),
        ],
        scratch_shapes=[pltpu.VMEM((rows - KEPT, width), queries.dtype), pltpu.SemaphoreType.DMA(())],
        compiler_params=grant(MIXED_MIB),
        cost_estimate=pl.CostEstimate(flops=2 * rows * HD * width, bytes_accessed=10 * rows * width, transcendentals=0),
        name="mixed",
    )(queries, top_queries, local, prefix, first)


def scored_kernel(mixed, squares, gain, out, rows, sems):
    total = squares[0]
    for p in range(1, PEERS):
        total = total + squares[p]
    scale = lax.rsqrt(total / D + 1e-06)
    copies = []
    for t in range(mixed.shape[0] // HD):
        at = slice(t * HD, (t + 1) * HD)
        column = jnp.swapaxes(jnp.broadcast_to(scale[t : t + 1], (HD, HD)), 0, 1)
        for h in range(mixed.shape[1] // HD):
            cols = head_columns(h)
            rows[at, cols] = (mixed[at, cols] * column * gain[:, cols]).astype(jnp.bfloat16)
        part = pl.ds(t * HD, HD)
        copies.append(pltpu.make_async_copy(rows.at[part], out.at[part], sems.at[t]))
        copies[-1].start()
    for copy in copies:
        copy.wait()


def scored_part(mixed, squares, gain):
    rows, width = mixed.shape
    return pl.pallas_call(
        scored_kernel,
        in_specs=[VMEM] * 3,
        out_specs=HBM,
        out_shape=jax.ShapeDtypeStruct((rows, width), jnp.bfloat16),
        scratch_shapes=[pltpu.VMEM((rows, width), jnp.bfloat16), pltpu.SemaphoreType.DMA((rows // HD,))],
        compiler_params=grant(OTHER_MIB),
        name="scored",
    )(mixed, squares, gain.reshape(1, width))


def shards(queries, keys, values, gain):
    total = shard_state(keys, values)
    prefix, (local, first, top_queries) = exclusive_states(total, functools.partial(local_part, queries, keys, values))
    mixed, squares = mixed_part(queries, top_queries, local, prefix, first)
    squares = lax.all_to_all(squares, "tp", 0, 0)
    return scored_part(mixed, squares, gain)


def solution(mesh):
    return jax.shard_map(
        shards,
        mesh=mesh,
        in_specs=(P("ctx", "tp"), P("ctx", "tp"), P("ctx", "tp"), P("tp")),
        out_specs=P("ctx", "tp"),
        check_vma=False,
    )
```
